32 devices in a mesh: grp: 4 (over y, core), dev: 8 (over z, x).
Axes of the slice: x: 2, y: 2, z: 4, core: 2. Of those that a mesh axis runs over, the one named last changes fastest.
Arguments:
- residual_edges: float32 [16, 172032], P(None, ('grp', 'dev')), may hold values from -6 to 6
- pi_block: float32 [144, 192], replicated, may hold values from -0.4375 to 0.4375
- stiff_block: float32 [64, 64], replicated, may hold values from -0.05 to 5.15, as said below
- mass_block: float32 [64, 64], replicated, may hold values from -0.03 to 3.89, as said below
- permittivity: float32 [6, 2048], P(None, ('grp', 'dev')), may hold values from -1.6 to 4, as said below
- curl_coef: float32 [2048], P(('grp', 'dev')), may hold values from 0.02 to 2
- edge_map: int32 [144, 2048], P(None, ('grp', 'dev')), may hold values from 0 to 6719, as said below
- local_map: int32 [64, 2048], P(None, ('grp', 'dev')), may hold values from 0 to 2047
- node_owner: int32 [65536], P(('grp', 'dev')), may hold values from 0 to 7, as said below
- node_slot: int32 [65536], P(('grp', 'dev')), may hold values from 0 to 1727
Outputs:
- correction: float32 [16, 172032], P(None, ('grp', 'dev'))
The draws below stay inside these ranges and needn't reach their ends.
Inputs may be any that keep to these rules, and one draw needn't show every extreme that they name: `edge_map`: entries of one device's elements (aligned blocks of 64 columns) below 672 or at 6048 or above occur only where the neighbouring block along grp+dev order exists; both ends of the range are reached wherever that neighbour exists. `node_owner`: among the 2048 touched nodes of one device at most 512 have the same owner; in every group one owner has exactly 512 from every device of that group. `stiff_block`: Symmetric; diagonal entries between 4.15 and 5.15, the others within 0.05 of zero. `mass_block`: Symmetric; diagonal entries between 2.89 and 3.89, the others within 0.03 of zero. `permittivity`: rows 0 to 2 lie between 0.05 and 4; rows 3 to 5 within 1.6 of zero.
All inputs are finite; a program needn't handle non-finite values.
Results may differ from the reference program's by a relative error of at most 0.0003.
Values sent between devices are 32-bit elements; how exact they have to be, the bound alone decides.
A program may use at most 128 MiB of HBM per device.

```python
import math
import jax
import jax.numpy as jnp
from jax import lax

RHS = 16
ED = 144
NN = 64
NC = 192
EL = 64
E_LOC = 5376
RIM = 672
N_LOC = 1728
U_LOC = 2048
ELEMS = 2048
EDGES = 172032
TOUCHED = 65536
N_DEV = 8


def symmetric_block(key, spread):
    upper = jax.random.uniform(key, (NN, NN), jnp.float32, -spread, spread)
    sym = 0.5 * (upper + upper.T)
    diag_key = jax.random.fold_in(key, 7)
    base = jax.random.uniform(diag_key, (NN,), jnp.float32, 1.0, 2.0) + spread * (NN - 1)
    return jnp.where(jnp.eye(NN, dtype=bool), base[:, None], sym)


def draw_stiff_block(key, part):
    key = jax.random.fold_in(key, 11)
    return symmetric_block(key, 0.05)


def draw_mass_block(key, part):
    key = jax.random.fold_in(key, 12)
    return symmetric_block(key, 0.03)


def draw_permittivity(key, part):
    key = jax.random.fold_in(key, 13)
    diag_key, off_key = jax.random.split(key)
    diag_part = jnp.exp(jax.random.uniform(diag_key, (3, ELEMS), jnp.float32, -2.9957323, 1.3862944))
    factor = jax.random.uniform(off_key, (3, ELEMS), jnp.float32, -0.4, 0.4)
    off_xy = factor[0] * jnp.sqrt(diag_part[0] * diag_part[1])
    off_xz = factor[1] * jnp.sqrt(diag_part[0] * diag_part[2])
    off_yz = factor[2] * jnp.sqrt(diag_part[1] * diag_part[2])
    return jnp.concatenate([diag_part, jnp.stack([off_xy, off_xz, off_yz], axis=0)], axis=0)


def draw_edge_map(key, part):
    key = jax.random.fold_in(key, 14)
    blocks = ELEMS // EL
    element = jnp.arange(ELEMS, dtype=jnp.int32)
    block = element // EL
    within = element % EL
    base_start = block * E_LOC
    own = jax.random.randint(jax.random.fold_in(key, 1), (ED, ELEMS), 0, E_LOC) + base_start[None, :]
    pick = jax.random.randint(jax.random.fold_in(key, 2), (ED, ELEMS), 0, 2) == 1
    depth = jax.random.randint(jax.random.fold_in(key, 3), (ED, ELEMS), 0, RIM)
    lower = base_start[None, :] - 1 - depth
    upper = base_start[None, :] + E_LOC + depth
    use_low = pick & ((within < EL // 4) & (block > 0))[None, :]
    use_up = pick & ((within >= EL - EL // 4) & (block < blocks - 1))[None, :]
    result = jnp.where(use_low, lower, jnp.where(use_up, upper, own))
    first_cond = (within == 0) & (block > 0)
    last_cond = (within == EL - 1) & (block < blocks - 1)
    top_row = jnp.where(first_cond, base_start - RIM, jnp.where(last_cond, base_start + E_LOC + RIM - 1, result[0]))
    result = result.at[0].set(top_row)
    return result - base_start[None, :] + RIM


def draw_node_owner(key, part):
    key = jax.random.fold_in(key, 15)
    blocks = TOUCHED // U_LOC
    capacity = 2 * U_LOC // N_DEV
    remain = U_LOC - capacity
    heavy_count = (N_DEV - 1) // 2
    light_count = N_DEV - 1 - heavy_count
    heavy_rows = 2 * remain // 3
    hot = jax.random.randint(jax.random.fold_in(key, 1), (blocks // N_DEV,), 0, N_DEV)
    hot_each = hot[jnp.arange(blocks, dtype=jnp.int32) // N_DEV]
    row_keys = jax.random.split(jax.random.fold_in(key, 2), blocks)
    row_perms = jax.vmap(lambda sub_key: jax.random.permutation(sub_key, U_LOC))(row_keys)
    peer_keys = jax.random.split(jax.random.fold_in(key, 3), blocks)
    peer_perms = jax.vmap(lambda sub_key: jax.random.permutation(sub_key, N_DEV - 1))(peer_keys)
    ranks = jnp.arange(U_LOC, dtype=jnp.int32)
    beyond = jnp.maximum(ranks - capacity, 0)
    place = jnp.where(beyond < heavy_rows, beyond % heavy_count, heavy_count + (beyond - heavy_rows) % light_count)
    others = jnp.take_along_axis(peer_perms, jnp.broadcast_to(place[None, :], (blocks, U_LOC)), axis=1)
    others = jnp.where(others >= hot_each[:, None], others + 1, others)
    ranked_owner = jnp.where(ranks[None, :] < capacity, hot_each[:, None], others)
    owner = jax.vmap(lambda perm_row, owner_row: jnp.zeros((U_LOC,), jnp.int32).at[perm_row].set(owner_row))(row_perms, ranked_owner)
    return owner.reshape(TOUCHED)


def set_ends(values, stream_key, low, largest):
    index_at = [jax.random.randint(jax.random.fold_in(stream_key, axis), (), 0, length) for axis, length in enumerate(values.shape)]
    main_axis = values.shape.index(max(values.shape))
    neighbour = index_at[:main_axis] + [(index_at[main_axis] + 1) % values.shape[main_axis]] + index_at[main_axis + 1:]
    return values.at[tuple(index_at)].set(low).at[tuple(neighbour)].set(largest)


def steps_of(own_key, extent, cuts, least, top_value):
    gain, own = 1.0, jax.random.fold_in(own_key, 6)
    for axis_at, parts in cuts:
        steps = jnp.exp(jax.random.uniform(jax.random.fold_in(own, axis_at), (parts,), jnp.float32, least / len(cuts), top_value / len(cuts)))
        gain = gain * jnp.repeat(steps, extent[axis_at] // parts).reshape([-1 if axis == axis_at else 1 for axis in range(len(extent))])
    return gain


def gaussian(stream_key, dims, deviation, reach, shards=(), kind=jnp.bfloat16):
    drawn = jax.random.normal(stream_key, dims, jnp.float32) * deviation
    if len(shards) > 0:
        drawn = steps_of(stream_key, dims, shards, -0.22, 0.18) * drawn
    return jnp.clip(drawn, min=-reach, max=reach).astype(kind)


def setup_inputs(seed: int = 0) -> dict:
    splits = jax.random.split(jax.random.key(seed), 11)
    residual_edges = gaussian(splits[0], (RHS, EDGES), 1.0, 6.0, ((1, 32),), jnp.float32)
    pi_block = gaussian(splits[1], (ED, NC), NC ** -0.5, 0.4375, (), jnp.float32)
    stiff_block = draw_stiff_block(jax.random.fold_in(splits[10], 71), 0)
    mass_block = draw_mass_block(jax.random.fold_in(splits[10], 71), 0)
    permittivity = draw_permittivity(jax.random.fold_in(splits[10], 71), 0)
    curl_coef = jnp.clip(jnp.exp(math.log(2.0) - 4.6051702 * jax.random.uniform(splits[5], (ELEMS,), jnp.float32) ** steps_of(splits[5], (ELEMS,), ((0, 32),), -0.2, 0.2)), 0.02, 2.0)
    edge_map = draw_edge_map(jax.random.fold_in(splits[10], 71), 0)
    local_map = set_ends(jax.random.randint(splits[7], (NN, ELEMS), 0, U_LOC), jax.random.fold_in(splits[7], 1), 0, U_LOC - 1).astype(jnp.int32)
    node_owner = draw_node_owner(jax.random.fold_in(splits[10], 71), 0)
    node_slot = set_ends(jax.random.randint(splits[9], (TOUCHED,), 0, N_LOC), jax.random.fold_in(splits[9], 1), 0, N_LOC - 1).astype(jnp.int32)
    return dict(residual_edges=residual_edges, pi_block=pi_block, stiff_block=stiff_block, mass_block=mass_block, permittivity=permittivity, curl_coef=curl_coef, edge_map=edge_map, local_map=local_map, node_owner=node_owner, node_slot=node_slot)


HIGH = lax.Precision.HIGHEST
CHEB_LOW = 0.3
CHEB_HIGH = 2.0


def cheb_factors():
    center = 0.5 * (CHEB_HIGH + CHEB_LOW)
    half_width = 0.5 * (CHEB_HIGH - CHEB_LOW)
    sigma_ratio = center / half_width
    rho_first = 1.0 / sigma_ratio
    rho_second = 1.0 / (2.0 * sigma_ratio - rho_first)
    return 1.0 / center, 1.0 + rho_second * rho_first, 2.0 * rho_second / half_width


def mixed_terms(stiff_part, mass_part, curl_scale, tensor):
    row_x = curl_scale * stiff_part[:, 0] + tensor[0] * mass_part[:, 0] + tensor[3] * mass_part[:, 1] + tensor[4] * mass_part[:, 2]
    row_y = curl_scale * stiff_part[:, 1] + tensor[3] * mass_part[:, 0] + tensor[1] * mass_part[:, 1] + tensor[5] * mass_part[:, 2]
    row_z = curl_scale * stiff_part[:, 2] + tensor[4] * mass_part[:, 0] + tensor[5] * mass_part[:, 1] + tensor[2] * mass_part[:, 2]
    return jnp.stack([row_x, row_y, row_z], axis=1)


def element_apply(values, stiff_block, mass_block, curl_scale, tensor):
    stiff_part = jnp.einsum("kj,rcje->rcke", stiff_block, values, precision=HIGH)
    mass_part = jnp.einsum("kj,rcje->rcke", mass_block, values, precision=HIGH)
    return mixed_terms(stiff_part, mass_part, curl_scale, tensor)


def diag_terms(stiff_block, mass_block, curl_scale, tensor):
    stiff_diag = jnp.diagonal(stiff_block)[:, None]
    mass_diag = jnp.diagonal(mass_block)[:, None]
    base = curl_scale[None, :] * stiff_diag
    return jnp.stack([base + mass_diag * tensor[0][None, :], base + mass_diag * tensor[1][None, :], base + mass_diag * tensor[2][None, :]], axis=0)


def reference(residual_edges, pi_block, stiff_block, mass_block, permittivity, curl_coef, edge_map, local_map, node_owner, node_slot):
    blocks = ELEMS // EL
    node_total = blocks * N_LOC
    holder = jnp.arange(TOUCHED, dtype=jnp.int32) // U_LOC
    global_ids = ((holder // N_DEV) * N_DEV + node_owner) * N_LOC + node_slot
    first, keep, step = cheb_factors()
    block_list = jnp.arange(blocks, dtype=jnp.int32)

    def block_data(block):
        offset = block * EL
        edges = lax.dynamic_slice_in_dim(edge_map, offset, EL, 1) + (block * E_LOC - RIM).astype(jnp.int32)
        local_ids = lax.dynamic_slice_in_dim(local_map, offset, EL, 1)
        node_ids = global_ids[block * U_LOC + local_ids]
        tensor = lax.dynamic_slice_in_dim(permittivity, offset, EL, 1)
        curl_scale = lax.dynamic_slice_in_dim(curl_coef, offset, EL, 0)
        return edges, node_ids, tensor, curl_scale

    def restrict(carry, block):
        node_sum, diag_sum = carry
        edges, node_ids, tensor, curl_scale = block_data(block)
        edge_values = residual_edges[:, edges]
        node_terms = jnp.einsum("dp,rde->rpe", pi_block, edge_values, precision=HIGH).reshape(RHS, 3, NN, EL)
        node_sum = node_sum.at[:, :, node_ids].add(node_terms)
        diag_sum = diag_sum.at[:, node_ids].add(diag_terms(stiff_block, mass_block, curl_scale, tensor))
        return (node_sum, diag_sum), None

    start_nodes = jnp.zeros((RHS, 3, node_total), jnp.float32)
    start_diag = jnp.zeros((3, node_total), jnp.float32)
    (rhs_nodes, diag_nodes), _ = lax.scan(restrict, (start_nodes, start_diag), block_list)
    floored = jnp.maximum(diag_nodes, 1.0)
    first_iter = first * rhs_nodes / floored[None]

    def operate(carry, block):
        edges, node_ids, tensor, curl_scale = block_data(block)
        values = first_iter[:, :, node_ids]
        return carry.at[:, :, node_ids].add(element_apply(values, stiff_block, mass_block, curl_scale, tensor)), None

    applied, _ = lax.scan(operate, jnp.zeros((RHS, 3, node_total), jnp.float32), block_list)
    second_iter = keep * first_iter + step * (rhs_nodes - applied) / floored[None]

    def prolong(carry, block):
        edges, node_ids, tensor, curl_scale = block_data(block)
        values = second_iter[:, :, node_ids].reshape(RHS, 3 * NN, EL)
        edge_terms = jnp.einsum("dp,rpe->rde", pi_block, values, precision=HIGH)
        return carry.at[:, edges].add(edge_terms), None

    correction, _ = lax.scan(prolong, jnp.zeros((RHS, EDGES), jnp.float32), block_list)
    return correction
```

```python
import functools
import jax
import jax.numpy as jnp
from jax import lax
from jax.experimental import pallas as pl
from jax.experimental.pallas import tpu as pltpu
from jax.sharding import PartitionSpec as P

N_LOC = 1728
CHUNK = 256
WIDE = 512
F32 = jnp.float32
BF16 = jnp.bfloat16
AUX = 8
CHEB_LOW = 0.3
CHEB_HIGH = 2.0
VMEM_BYTES = 50 * 1024 * 1024


def cheb_factors():
    center = 0.5 * (CHEB_HIGH + CHEB_LOW)
    half_width = 0.5 * (CHEB_HIGH - CHEB_LOW)
    sigma_ratio = center / half_width
    rho_first = 1.0 / sigma_ratio
    rho_second = 1.0 / (2.0 * sigma_ratio - rho_first)
    return (1.0 / center, 1.0 + rho_second * rho_first, 2.0 * rho_second / half_width)


def iota(shape, dim):
    return lax.broadcasted_iota(jnp.int32, shape, dim)


def dot(a, b):
    return lax.dot_general(a, b, (((1,), (0,)), ((), ())), preferred_element_type=F32)


def dot_nt(a, b):
    return lax.dot_general(a, b, (((1,), (1,)), ((), ())), preferred_element_type=F32)


def split(x):
    high = x.astype(BF16)
    low = (x - high.astype(F32)).astype(BF16)
    return high, low


def split_wide(x):
    high, low = split(x)
    return jnp.concatenate([high, low], axis=1)


def ones_where(mask):
    return jnp.where(mask, 1.0, 0.0).astype(BF16)


def onehot(low_index):
    return ones_where(iota((CHUNK, low_index.shape[1]), 0) == low_index)


def gather_cols(table2, high_index, hot, groups, rows):
    found = dot(table2, jnp.concatenate([hot, hot], axis=0))
    picked = jnp.zeros((rows, hot.shape[1]), F32)
    for h in range(groups):
        picked = jnp.where(high_index == h, found[h * rows : (h + 1) * rows], picked)
    return picked


def scatter_cols(values, high_index, hot, groups):
    high, low = split(values)
    high, low = high.astype(F32), low.astype(F32)
    masks = [high_index == h for h in range(groups)]
    high_rows = jnp.concatenate([jnp.where(m, high, 0.0) for m in masks], axis=0)
    low_rows = jnp.concatenate([jnp.where(m, low, 0.0) for m in masks], axis=0)
    both = jnp.concatenate([high_rows.astype(BF16), low_rows.astype(BF16)], axis=1)
    return dot_nt(both, jnp.concatenate([hot, hot], axis=1))


def dot3(x, w_high, w_low):
    high, low = split(x)
    return dot(high, w_high) + dot(low, w_high) + dot(high, w_low)


def dot3_nt(x, w_high, w_low):
    high, low = split(x)
    return dot_nt(high, w_high) + dot_nt(low, w_high) + dot_nt(high, w_low)


def block_weights(block, copies):
    size = block.shape[0]
    total = size * copies
    spread = ones_where(iota((size, total), 1) % size == iota((size, total), 0))
    keep = iota((total, total), 0) // size == iota((total, total), 1) // size
    out = []
    for part in split(block):
        row = dot(part, spread)
        full = jnp.concatenate([row] * copies, axis=0)
        out.append(jnp.where(keep, full, 0.0).astype(BF16))
    return out


def pi_weights(pi_rows, copies, nodes):
    count, total = pi_rows.shape
    comps = total // nodes
    width = comps * copies * nodes
    col, row = iota((total, width), 1), iota((total, width), 0)
    per = copies * nodes
    spread = ones_where((col // per == row // nodes) & (col % nodes == row % nodes))
    shape = (copies * count, width)
    keep = iota(shape, 0) // count == (iota(shape, 1) % per) // nodes
    out = []
    for part in split(pi_rows):
        one = dot(part, spread)
        full = jnp.concatenate([one] * copies, axis=0)
        out.append(jnp.where(keep, full, 0.0).astype(BF16))
    return out


def prepare_weights(pi_ref, stiff_ref, mass_ref, wa, wb, ws, wm):
    nodes = stiff_ref.shape[0]
    for ref, parts in (
        (wa, pi_weights(pi_ref[:128], 2, nodes)),
        (wb, pi_weights(pi_ref[128:], 8, nodes)),
        (ws, block_weights(stiff_ref[...], 4)),
        (wm, block_weights(mass_ref[...], 4)),
    ):
        ref[0] = parts[0]
        ref[1] = parts[1]


def prepare_coefs(coef_ref, stiff_ref, mass_ref, coef_q, diag_q):
    nodes = stiff_ref.shape[0]
    eye = iota((nodes, nodes), 0) == iota((nodes, nodes), 1)
    sd = jnp.sum(jnp.where(eye, stiff_ref[...], 0.0), axis=0, keepdims=True)
    md = jnp.sum(jnp.where(eye, mass_ref[...], 0.0), axis=0, keepdims=True)
    diags = jnp.concatenate([sd, md, jnp.zeros((6, nodes), F32)], axis=0)
    d_parts = split(diags)
    c_parts = split(coef_ref[...])
    elems = coef_ref.shape[1]

    def body(i, _):
        lane = iota((elems, WIDE), 1) + i * WIDE
        by_elem = ones_where(lane // nodes == iota((elems, WIDE), 0))
        lane_n = iota((nodes, WIDE), 1)
        by_node = ones_where(lane_n % nodes == iota((nodes, WIDE), 0))
        coef = dot(c_parts[0], by_elem) + dot(c_parts[1], by_elem)
        diag = dot(d_parts[0], by_node) + dot(d_parts[1], by_node)
        at = pl.ds(pl.multiple_of(i * WIDE, WIDE), WIDE)
        coef_q[:, at] = coef
        base = coef[0:1] * diag[0:1]
        rows = iota((AUX, WIDE), 0)
        terms = jnp.zeros((AUX, WIDE), F32)
        for c in range(3):
            terms = jnp.where(rows == c, base + diag[1:2] * coef[1 + c : 2 + c], terms)
        diag_q[:, at] = terms
        return 0

    lax.fori_loop(0, coef_q.shape[1] // WIDE, body, 0)


def prepare_places(peers, owner_ref, slot_ref, local_ref, pos_hi, pos_lo, slot_buf):
    touched = owner_ref.shape[1]
    capacity = 2 * touched // peers
    groups = 2 * touched // CHUNK
    tri = ones_where(iota((CHUNK, CHUNK), 0) < iota((CHUNK, CHUNK), 1))
    carry = jnp.zeros((peers, 1), F32)
    place = []
    for i in range(touched // CHUNK):
        own = owner_ref[:, i * CHUNK : (i + 1) * CHUNK]
        hot = jnp.where(iota((peers, CHUNK), 0) == own, 1.0, 0.0)
        before = dot(hot.astype(BF16), tri) + carry
        rank = jnp.sum(hot * before, axis=0, keepdims=True)
        carry = carry + jnp.sum(hot, axis=1, keepdims=True)
        place.append(own * capacity + rank.astype(jnp.int32))
    rows8 = iota((AUX, CHUNK), 0)
    table_hi = jnp.zeros((AUX, CHUNK), F32)
    table_lo = jnp.zeros((AUX, CHUNK), F32)
    slots = jnp.zeros((2 * groups, CHUNK), F32)
    for i, pos in enumerate(place):
        high, low = pos // CHUNK, pos % CHUNK
        table_hi = jnp.where(rows8 == i, high.astype(F32), table_hi)
        table_lo = jnp.where(rows8 == i, low.astype(F32), table_lo)
        slot = slot_ref[:, i * CHUNK : (i + 1) * CHUNK] + 1
        here = iota((groups, CHUNK), 0) == high
        s_hi = jnp.where(here, (slot // CHUNK).astype(F32), 0.0)
        s_lo = jnp.where(here, (slot % CHUNK).astype(F32), 0.0)
        both = jnp.concatenate([s_hi, s_lo], axis=0).astype(BF16)
        slots = slots + dot_nt(both, onehot(low))
    slot_buf[...] = slots[:groups] * float(CHUNK) + slots[groups:]
    table = jnp.concatenate([table_hi, table_lo], axis=0).astype(BF16)

    def body(i, _):
        at = pl.ds(pl.multiple_of(i * WIDE, WIDE), WIDE)
        local = local_ref[:, at]
        found = dot(table, onehot(local % CHUNK))
        here = iota((AUX, WIDE), 0) == local // CHUNK
        high = jnp.sum(jnp.where(here, found[:AUX], 0.0), axis=0, keepdims=True)
        low = jnp.sum(jnp.where(here, found[AUX:], 0.0), axis=0, keepdims=True)
        pos_hi[:, at] = high.astype(jnp.int32)
        pos_lo[:, at] = low.astype(jnp.int32)
        return 0

    lax.fori_loop(0, local_ref.shape[1] // WIDE, body, 0)


def edge_gather(table2, emap_ref, rhs, xa, xb):
    groups = table2.shape[0] // rhs
    a_chunks = xa.shape[0] // rhs * CHUNK // WIDE

    def take(i):
        at = pl.ds(pl.multiple_of(i * WIDE, WIDE), WIDE)
        index = emap_ref[:, at]
        return gather_cols(table2[...], index // CHUNK, onehot(index % CHUNK), groups, rhs)

    def body(i, _):
        got = take(i)
        for s in range(2):
            at = pl.multiple_of((2 * i + s) * rhs, rhs)
            xa[pl.ds(at, rhs), :] = got[:, s * CHUNK : (s + 1) * CHUNK]
        return 0

    lax.fori_loop(0, a_chunks, body, 0)
    for i in range(2):
        got = take(a_chunks + i)
        for s in range(4):
            xb[(4 * i + s) * rhs : (4 * i + s + 1) * rhs, :] = got[:, s * 128 : (s + 1) * 128]


def restrict(xa, xb, wa, wb, rhs, terms):
    ya = dot3(xa[...], wa[0], wa[1])
    yb = dot3(xb[...], wb[0], wb[1])
    for p in range(xa.shape[0] // rhs):
        for c in range(3):
            first = ya[p * rhs : (p + 1) * rhs, c * 128 : (c + 1) * 128]
            lane = c * 512 + (p % 4) * 128
            second = yb[(p // 4) * rhs : (p // 4 + 1) * rhs, lane : lane + 128]
            terms[c * rhs : (c + 1) * rhs, p * 128 : (p + 1) * 128] = first + second


def scatter_elems(terms, pos_hi, pos_lo, acc):
    rows, total = terms.shape
    groups = acc.shape[0] // rows
    acc[...] = jnp.zeros_like(acc)

    def body(i, _):
        at = pl.ds(pl.multiple_of(i * WIDE, WIDE), WIDE)
        acc[...] += scatter_cols(terms[:, at], pos_hi[:, at], onehot(pos_lo[:, at]), groups)
        return 0

    lax.fori_loop(0, total // WIDE, body, 0)


def lay_out(send, acc, rows, first_row):
    capacity = send.shape[2]
    for h in range(acc.shape[0] // rows):
        step = min(capacity, CHUNK)
        for s in range(CHUNK // step):
            lane = h * CHUNK + s * step
            peer, off = lane // capacity, lane % capacity
            send[peer, first_row : first_row + rows, off : off + step] = acc[
                h * rows : (h + 1) * rows, s * step : (s + 1) * step
            ]


def table_from(got, rows, table2):
    peers, _, capacity = got.shape
    for h in range(peers * capacity // CHUNK):
        step = min(capacity, CHUNK)
        parts = []
        for s in range(CHUNK // step):
            lane = h * CHUNK + s * step
            peer, off = lane // capacity, lane % capacity
            parts.append(got[peer, :rows, off : off + step])
        value = parts[0] if len(parts) == 1 else jnp.concatenate(parts, axis=1)
        table2[h * rows : (h + 1) * rows, :] = split_wide(value)


def gather_elems(table2, pos_hi, pos_lo, rows, visit):
    groups = table2.shape[0] // rows

    def body(i, _):
        at = pl.ds(pl.multiple_of(i * WIDE, WIDE), WIDE)
        visit(i, gather_cols(table2[...], pos_hi[:, at], onehot(pos_lo[:, at]), groups, rows))
        return 0

    lax.fori_loop(0, pos_hi.shape[1] // WIDE, body, 0)


def home_index(slot_row):
    slot = slot_row.astype(jnp.int32) - 1
    return jnp.where(slot < 0, -1, slot // CHUNK), jnp.maximum(slot, 0) % CHUNK


def sum_home(got, slots, first_row, rows, acc):
    groups = acc.shape[0] // rows
    acc[...] = jnp.zeros_like(acc)

    def body(p, _):
        high, low = home_index(slots[p])
        values = got[p, first_row : first_row + rows, :]
        acc[...] += scatter_cols(values, high, onehot(low), groups)
        return 0

    lax.fori_loop(0, got.shape[0], body, 0)


def fetch_home(table2, slots, rows, send):
    groups = table2.shape[0] // rows

    def body(p, _):
        high, low = home_index(slots[p])
        send[p] = gather_cols(table2[...], high, onehot(low), groups, rows)
        return 0

    lax.fori_loop(0, send.shape[0], body, 0)


def apply_operator(x_all, ws, wm, coef_q, rhs, terms):
    rows = 3 * rhs
    stiff = dot3(x_all[...], ws[0], ws[1])
    mass = dot3(x_all[...], wm[0], wm[1])
    tensor = ((1, 4, 5), (4, 2, 6), (5, 6, 3))
    for i in range(x_all.shape[0] // rows):
        lanes = slice(i * CHUNK, (i + 1) * CHUNK)
        coef = coef_q[:, lanes]
        for c in range(3):
            at = i * rows + c * rhs
            total = coef[0:1] * stiff[at : at + rhs]
            for c2 in range(3):
                t = tensor[c][c2]
                at2 = i * rows + c2 * rhs
                total = total + coef[t : t + 1] * mass[at2 : at2 + rhs]
            terms[c * rhs : (c + 1) * rhs, lanes] = total


def edge_scatter(ea, eb, emap_ref, rhs, acc):
    groups = acc.shape[0] // rhs
    a_chunks = ea.shape[0] // rhs * CHUNK // WIDE
    acc[...] = jnp.zeros_like(acc)

    def put(i, values):
        at = pl.ds(pl.multiple_of(i * WIDE, WIDE), WIDE)
        index = emap_ref[:, at]
        acc[...] += scatter_cols(values, index // CHUNK, onehot(index % CHUNK), groups)

    def body(i, _):
        parts = [ea[pl.ds(pl.multiple_of((2 * i + s) * rhs, rhs), rhs), :] for s in range(2)]
        put(i, jnp.concatenate(parts, axis=1))
        return 0

    lax.fori_loop(0, a_chunks, body, 0)
    for i in range(2):
        parts = [eb[(4 * i + s) * rhs : (4 * i + s + 1) * rhs, :] for s in range(4)]
        put(a_chunks + i, jnp.concatenate(parts, axis=1))


def restrict_kernel(
    peers, res, before, after, emap, local, owner, slot, coef, pi, stiff, mass,
    send, pos_hi, pos_lo, coef_q, wa, wb, ws, wm,
    table2, xa, xb, terms, diag_q, acc, acc_d, slot_buf,
):
    rhs = res.shape[0]
    prepare_weights(pi, stiff, mass, wa, wb, ws, wm)
    prepare_coefs(coef, stiff, mass, coef_q, diag_q)
    prepare_places(peers, owner, slot, local, pos_hi, pos_lo, slot_buf)
    h = 0
    for ref in (res, before, after):
        for i in range(ref.shape[1] // CHUNK):
            table2[h * rhs : (h + 1) * rhs, :] = split_wide(ref[:, i * CHUNK : (i + 1) * CHUNK])
            h += 1
    edge_gather(table2, emap, rhs, xa, xb)
    restrict(xa, xb, wa, wb, rhs, terms)
    scatter_elems(terms, pos_hi, pos_lo, acc)
    scatter_elems(diag_q, pos_hi, pos_lo, acc_d)
    for g in range(slot_buf.shape[0]):
        acc_d[g * AUX + 3 : g * AUX + 4, :] = slot_buf[g : g + 1, :]
    lay_out(send, acc, 3 * rhs, 0)
    lay_out(send, acc_d, AUX, 3 * rhs)


def first_home(got, send, slots, rhs_nodes, floored, acc_d, table2):
    rows = send.shape[1]
    rhs = rows // 3
    first = cheb_factors()[0]
    slots[...] = got[:, rows + 3 : rows + 4, :]
    sum_home(got, slots, 0, rows, rhs_nodes)
    sum_home(got, slots, rows, AUX, acc_d)
    floored[...] = jnp.maximum(acc_d[...], 1.0)
    for h in range(rhs_nodes.shape[0] // rows):
        for c in range(3):
            at = slice(h * rows + c * rhs, h * rows + (c + 1) * rhs)
            weight = floored[h * AUX + c : h * AUX + c + 1, :]
            table2[at, :] = split_wide(first * rhs_nodes[at, :] / weight)
    fetch_home(table2, slots, rows, send)


def second_home(got, slots, rhs_nodes, floored, send, acc, table2):
    rows = send.shape[1]
    rhs = rows // 3
    first, keep, step = cheb_factors()
    sum_home(got, slots, 0, rows, acc)
    for h in range(rhs_nodes.shape[0] // rows):
        for c in range(3):
            at = slice(h * rows + c * rhs, h * rows + (c + 1) * rhs)
            weight = floored[h * AUX + c : h * AUX + c + 1, :]
            nodes = rhs_nodes[at, :]
            value = keep * (first * nodes / weight) + step * (nodes - acc[at, :]) / weight
            table2[at, :] = split_wide(value)
    fetch_home(table2, slots, rows, send)


def operate_kernel(got, pos_hi, pos_lo, coef_q, ws, wm, send, table2, x_all, terms, acc):
    rows = send.shape[1]
    table_from(got, rows, table2)

    def visit(i, value):
        for s in range(2):
            at = pl.multiple_of((2 * i + s) * rows, rows)
            x_all[pl.ds(at, rows), :] = value[:, s * CHUNK : (s + 1) * CHUNK]

    gather_elems(table2, pos_hi, pos_lo, rows, visit)
    apply_operator(x_all, ws, wm, coef_q, rows // 3, terms)
    scatter_elems(terms, pos_hi, pos_lo, acc)
    lay_out(send, acc, rows, 0)


def prolong_kernel(
    got, pos_hi, pos_lo, emap, wa, wb, own, before, after, table2, xa, xb, ea, eb, acc
):
    rows = got.shape[1]
    rhs = rows // 3
    table_from(got, rows, table2)

    def visit(i, value):
        for c in range(3):
            part = value[c * rhs : (c + 1) * rhs]
            xb[pl.ds(pl.multiple_of(i * rhs, rhs), rhs), c * WIDE : (c + 1) * WIDE] = part
            for s in range(4):
                at = pl.multiple_of((4 * i + s) * rhs, rhs)
                xa[pl.ds(at, rhs), c * 128 : (c + 1) * 128] = part[:, s * 128 : (s + 1) * 128]

    gather_elems(table2, pos_hi, pos_lo, rows, visit)
    ea[...] = dot3_nt(xa[...], wa[0], wa[1])
    eb[...] = dot3_nt(xb[...], wb[0], wb[1])
    edge_scatter(ea, eb, emap, rhs, acc)
    h = 0
    for ref in (own, before, after):
        for i in range(ref.shape[1] // CHUNK):
            ref[:, i * CHUNK : (i + 1) * CHUNK] = acc[h * rhs : (h + 1) * rhs, :]
            h += 1


def call(body, outs, scratch, *args):
    vmem = pl.BlockSpec(memory_space=pltpu.VMEM)
    return pl.pallas_call(
        body,
        out_shape=[jax.ShapeDtypeStruct(*o) for o in outs],
        in_specs=[vmem] * len(args),
        out_specs=[vmem] * len(outs),
        scratch_shapes=[pltpu.VMEM(*s) for s in scratch],
        compiler_params=pltpu.CompilerParams(vmem_limit_bytes=VMEM_BYTES),
    )(*args)


def shifted(array, width_axes, up):
    size = lax.axis_size(width_axes)
    pairs = [(i, i + 1) for i in range(size - 1)]
    return lax.ppermute(array, width_axes, pairs if up else [(j, i) for i, j in pairs])


def per_device(
    residual, pi, stiff, mass, permittivity, curl, edge_map, local_map, node_owner, node_slot
):
    rhs, edges = residual.shape
    ed, elems = edge_map.shape
    nodes = local_map.shape[0]
    touched = node_owner.shape[0]
    peers = lax.axis_size("dev")
    capacity = 2 * touched // peers
    rim = edges // 8
    rim_pad = -(-rim // CHUNK) * CHUNK
    rows = 3 * rhs
    entries = nodes * elems
    e_entries = ed * elems
    axes = ("grp", "dev")
    pad = ((0, 0), (0, rim_pad - rim))
    before = jnp.pad(shifted(residual[:, edges - rim :], axes, True), pad)
    after = jnp.pad(shifted(residual[:, :rim], axes, False), pad)
    place = edge_map.T - rim
    place = jnp.where(
        place < 0,
        place + rim + edges,
        jnp.where(place >= edges, place + rim_pad, place),
    )
    emap = jnp.concatenate([place[:, :128].reshape(1, -1), place[:, 128:].reshape(1, -1)], axis=1)
    local = local_map.T.reshape(1, -1)
    coef = jnp.concatenate([curl[None], permittivity, jnp.zeros((1, elems), F32)], axis=0)
    groups = 2 * touched // CHUNK
    home = -(-N_LOC // CHUNK)
    e_groups = (edges + 2 * rim_pad) // CHUNK
    pairs = elems // 2
    buffer = ((peers, rows, capacity), F32)
    wa_shape, wb_shape = ((2, 256, 384), BF16), ((2, 128, 1536), BF16)
    ws_shape = ((2, CHUNK, CHUNK), BF16)
    send, pos_hi, pos_lo, coef_q, wa, wb, ws, wm = call(
        functools.partial(restrict_kernel, peers),
        [
            ((peers, rows + AUX, capacity), F32),
            ((1, entries), jnp.int32),
            ((1, entries), jnp.int32),
            ((AUX, entries), F32),
            wa_shape, wb_shape, ws_shape, ws_shape,
        ],
        [
            ((e_groups * rhs, 2 * CHUNK), BF16),
            ((pairs * rhs, 256), F32),
            ((elems // 8 * rhs, 128), F32),
            ((rows, entries), F32),
            ((AUX, entries), F32),
            ((groups * rows, CHUNK), F32),
            ((groups * AUX, CHUNK), F32),
            ((groups, CHUNK), F32),
        ],
        residual, before, after, emap, local, node_owner[None], node_slot[None], coef, pi, stiff,
        mass,
    )

    def exchange(array):
        return lax.all_to_all(array, "dev", split_axis=0, concat_axis=0, tiled=True)

    send, slots, rhs_nodes, floored = call(
        first_home,
        [
            buffer,
            ((peers, 1, capacity), F32),
            ((home * rows, CHUNK), F32),
            ((home * AUX, CHUNK), F32),
        ],
        [((home * AUX, CHUNK), F32), ((home * rows, 2 * CHUNK), BF16)],
        exchange(send),
    )
    (send,) = call(
        operate_kernel,
        [buffer],
        [
            ((groups * rows, 2 * CHUNK), BF16),
            ((entries // CHUNK * rows, CHUNK), F32),
            ((rows, entries), F32),
            ((groups * rows, CHUNK), F32),
        ],
        exchange(send), pos_hi, pos_lo, coef_q, ws, wm,
    )
    (send,) = call(
        second_home,
        [buffer],
        [((home * rows, CHUNK), F32), ((home * rows, 2 * CHUNK), BF16)],
        exchange(send), slots, rhs_nodes, floored,
    )
    own, to_before, to_after = call(
        prolong_kernel,
        [((rhs, edges), F32), ((rhs, rim_pad), F32), ((rhs, rim_pad), F32)],
        [
            ((groups * rows, 2 * CHUNK), BF16),
            ((pairs * rhs, 384), F32),
            ((elems // 8 * rhs, 1536), F32),
            ((pairs * rhs, 256), F32),
            ((elems // 8 * rhs, 128), F32),
            ((e_groups * rhs, CHUNK), F32),
        ],
        exchange(send), pos_hi, pos_lo, emap, wa, wb,
    )
    from_after = shifted(to_before[:, :rim], axes, False)
    from_before = shifted(to_after[:, :rim], axes, True)
    own = own.at[:, :rim].add(from_before)
    return own.at[:, edges - rim :].add(from_after)


def solution(mesh):
    both = ("grp", "dev")
    in_specs = (
        P(None, both), P(), P(), P(), P(None, both), P(both), P(None, both), P(None, both),
        P(both), P(both),
    )
    return jax.shard_map(
        per_device, mesh=mesh, in_specs=in_specs, out_specs=P(None, both), check_vma=False
    )
```

```python
import functools
import jax
import jax.numpy as jnp
from jax import lax
from jax.experimental import pallas as pl
from jax.experimental.pallas import tpu as pltpu
from jax.sharding import PartitionSpec as P

N_LOC = 1728
CHUNK = 256
WIDE = 512
F32 = jnp.float32
BF16 = jnp.bfloat16
AUX = 8
CHEB_LOW = 0.3
CHEB_HIGH = 2.0
VMEM_BYTES = 50 * 1024 * 1024


def cheb_factors():
    center = 0.5 * (CHEB_HIGH + CHEB_LOW)
    half_width = 0.5 * (CHEB_HIGH - CHEB_LOW)
    sigma_ratio = center / half_width
    rho_first = 1.0 / sigma_ratio
    rho_second = 1.0 / (2.0 * sigma_ratio - rho_first)
    return (1.0 / center, 1.0 + rho_second * rho_first, 2.0 * rho_second / half_width)


def iota(shape, dim):
    return lax.broadcasted_iota(jnp.int32, shape, dim)


def dot(a, b):
    return lax.dot_general(a, b, (((1,), (0,)), ((), ())), preferred_element_type=F32)


def dot_nt(a, b):
    return lax.dot_general(a, b, (((1,), (1,)), ((), ())), preferred_element_type=F32)


def split(x):
    high = x.astype(BF16)
    low = (x - high.astype(F32)).astype(BF16)
    return high, low


def split_wide(x):
    high, low = split(x)
    return jnp.concatenate([high, low], axis=1)


def ones_where(mask):
    return jnp.where(mask, 1.0, 0.0).astype(BF16)


def onehot(low_index):
    return ones_where(iota((CHUNK, low_index.shape[1]), 0) == low_index)


def gather_cols(table2, high_index, hot, groups, rows):
    found = dot(table2, jnp.concatenate([hot, hot], axis=0))
    picked = jnp.zeros((rows, hot.shape[1]), F32)
    for h in range(groups):
        picked = jnp.where(high_index == h, found[h * rows : (h + 1) * rows], picked)
    return picked


def scatter_cols(values, high_index, hot, groups):
    high, low = split(values)
    high, low = high.astype(F32), low.astype(F32)
    masks = [high_index == h for h in range(groups)]
    high_rows = jnp.concatenate([jnp.where(m, high, 0.0) for m in masks], axis=0)
    low_rows = jnp.concatenate([jnp.where(m, low, 0.0) for m in masks], axis=0)
    both = jnp.concatenate([high_rows.astype(BF16), low_rows.astype(BF16)], axis=1)
    return dot_nt(both, jnp.concatenate([hot, hot], axis=1))


def dot3(x, w_high, w_low):
    high, low = split(x)
    return dot(high, w_high) + dot(low, w_high) + dot(high, w_low)


def dot3_nt(x, w_high, w_low):
    high, low = split(x)
    return dot_nt(high, w_high) + dot_nt(low, w_high) + dot_nt(high, w_low)


def block_weights(block, copies):
    size = block.shape[0]
    total = size * copies
    spread = ones_where(iota((size, total), 1) % size == iota((size, total), 0))
    keep = iota((total, total), 0) // size == iota((total, total), 1) // size
    out = []
    for part in split(block):
        row = dot(part, spread)
        full = jnp.concatenate([row] * copies, axis=0)
        out.append(jnp.where(keep, full, 0.0).astype(BF16))
    return out


def pi_weights(pi_rows, copies, nodes):
    count, total = pi_rows.shape
    comps = total // nodes
    width = comps * copies * nodes
    col, row = iota((total, width), 1), iota((total, width), 0)
    per = copies * nodes
    spread = ones_where((col // per == row // nodes) & (col % nodes == row % nodes))
    shape = (copies * count, width)
    keep = iota(shape, 0) // count == (iota(shape, 1) % per) // nodes
    out = []
    for part in split(pi_rows):
        one = dot(part, spread)
        full = jnp.concatenate([one] * copies, axis=0)
        out.append(jnp.where(keep, full, 0.0).astype(BF16))
    return out


def keep_parts(ref, parts):
    ref[0] = parts[0]
    ref[1] = parts[1]


def prepare_coefs(coef_ref, stiff_ref, mass_ref, coef_q, diag_q):
    nodes = stiff_ref.shape[0]
    eye = iota((nodes, nodes), 0) == iota((nodes, nodes), 1)
    sd = jnp.sum(jnp.where(eye, stiff_ref[...], 0.0), axis=0, keepdims=True)
    md = jnp.sum(jnp.where(eye, mass_ref[...], 0.0), axis=0, keepdims=True)
    diags = jnp.concatenate([sd, md, jnp.zeros((6, nodes), F32)], axis=0)
    d_parts = split(diags)
    c_parts = split(coef_ref[...])
    elems = coef_ref.shape[1]

    def body(i, _):
        lane = iota((elems, WIDE), 1) + i * WIDE
        by_elem = ones_where(lane // nodes == iota((elems, WIDE), 0))
        lane_n = iota((nodes, WIDE), 1)
        by_node = ones_where(lane_n % nodes == iota((nodes, WIDE), 0))
        coef = dot(c_parts[0], by_elem) + dot(c_parts[1], by_elem)
        diag = dot(d_parts[0], by_node) + dot(d_parts[1], by_node)
        at = pl.ds(pl.multiple_of(i * WIDE, WIDE), WIDE)
        coef_q[:, at] = coef
        base = coef[0:1] * diag[0:1]
        rows = iota((AUX, WIDE), 0)
        terms = jnp.zeros((AUX, WIDE), F32)
        for c in range(3):
            terms = jnp.where(rows == c, base + diag[1:2] * coef[1 + c : 2 + c], terms)
        diag_q[:, at] = terms
        return 0

    lax.fori_loop(0, coef_q.shape[1] // WIDE, body, 0)


def prepare_places(peers, owner_ref, slot_ref, local_ref, pos_hi, hot_el, slot_buf):
    touched = owner_ref.shape[1]
    capacity = 2 * touched // peers
    groups = 2 * touched // CHUNK
    tri = ones_where(iota((CHUNK, CHUNK), 0) < iota((CHUNK, CHUNK), 1))
    carry = jnp.zeros((peers, 1), F32)
    place = []
    for i in range(touched // CHUNK):
        own = owner_ref[:, i * CHUNK : (i + 1) * CHUNK]
        hot = jnp.where(iota((peers, CHUNK), 0) == own, 1.0, 0.0)
        before = dot(hot.astype(BF16), tri) + carry
        rank = jnp.sum(hot * before, axis=0, keepdims=True)
        carry = carry + jnp.sum(hot, axis=1, keepdims=True)
        place.append(own * capacity + rank.astype(jnp.int32))
    rows8 = iota((AUX, CHUNK), 0)
    table_hi = jnp.zeros((AUX, CHUNK), F32)
    table_lo = jnp.zeros((AUX, CHUNK), F32)
    slots = jnp.zeros((2 * groups, CHUNK), F32)
    for i, pos in enumerate(place):
        high, low = pos // CHUNK, pos % CHUNK
        table_hi = jnp.where(rows8 == i, high.astype(F32), table_hi)
        table_lo = jnp.where(rows8 == i, low.astype(F32), table_lo)
        slot = slot_ref[:, i * CHUNK : (i + 1) * CHUNK] + 1
        here = iota((groups, CHUNK), 0) == high
        s_hi = jnp.where(here, (slot // CHUNK).astype(F32), 0.0)
        s_lo = jnp.where(here, (slot % CHUNK).astype(F32), 0.0)
        both = jnp.concatenate([s_hi, s_lo], axis=0).astype(BF16)
        slots = slots + dot_nt(both, onehot(low))
    slot_buf[...] = slots[:groups] * float(CHUNK) + slots[groups:]
    table = jnp.concatenate([table_hi, table_lo], axis=0).astype(BF16)

    def body(i, _):
        at = pl.ds(pl.multiple_of(i * WIDE, WIDE), WIDE)
        local = local_ref[:, at]
        found = dot(table, onehot(local % CHUNK))
        here = iota((AUX, WIDE), 0) == local // CHUNK
        high = jnp.sum(jnp.where(here, found[:AUX], 0.0), axis=0, keepdims=True)
        low = jnp.sum(jnp.where(here, found[AUX:], 0.0), axis=0, keepdims=True)
        pos_hi[:, at] = high.astype(jnp.int32)
        hot_el[:, at] = onehot(low.astype(jnp.int32))
        return 0

    lax.fori_loop(0, local_ref.shape[1] // WIDE, body, 0)


def edge_gather(table2, emap_hi, hot_ed, groups, rhs, xa, xb):
    a_chunks = xa.shape[0] // rhs * CHUNK // WIDE

    def take(i):
        at = pl.ds(pl.multiple_of(i * WIDE, WIDE), WIDE)
        return gather_cols(table2[...], emap_hi[:, at], hot_ed[:, at], groups, rhs)

    def body(i, _):
        got = take(i)
        for s in range(2):
            at = pl.multiple_of((2 * i + s) * rhs, rhs)
            xa[pl.ds(at, rhs), :] = got[:, s * CHUNK : (s + 1) * CHUNK]
        return 0

    lax.fori_loop(0, a_chunks, body, 0)
    for i in range(2):
        got = take(a_chunks + i)
        for s in range(4):
            xb[(4 * i + s) * rhs : (4 * i + s + 1) * rhs, :] = got[:, s * 128 : (s + 1) * 128]


def restrict(xa, xb, wa, wb, rhs, terms):
    ya = dot3(xa[...], wa[0], wa[1])
    yb = dot3(xb[...], wb[0], wb[1])
    for p in range(xa.shape[0] // rhs):
        for c in range(3):
            first = ya[p * rhs : (p + 1) * rhs, c * 128 : (c + 1) * 128]
            lane = c * 512 + (p % 4) * 128
            second = yb[(p // 4) * rhs : (p // 4 + 1) * rhs, lane : lane + 128]
            terms[c * rhs : (c + 1) * rhs, p * 128 : (p + 1) * 128] = first + second


def scatter_elems(terms, pos_hi, hot_el, acc):
    rows, total = terms.shape
    groups = acc.shape[0] // rows
    acc[...] = jnp.zeros_like(acc)

    def body(i, _):
        at = pl.ds(pl.multiple_of(i * WIDE, WIDE), WIDE)
        acc[...] += scatter_cols(terms[:, at], pos_hi[:, at], hot_el[:, at], groups)
        return 0

    lax.fori_loop(0, total // WIDE, body, 0)


def lay_out(send, acc, rows, first_row):
    capacity = send.shape[2]
    for h in range(acc.shape[0] // rows):
        step = min(capacity, CHUNK)
        for s in range(CHUNK // step):
            lane = h * CHUNK + s * step
            peer, off = lane // capacity, lane % capacity
            send[peer, first_row : first_row + rows, off : off + step] = acc[
                h * rows : (h + 1) * rows, s * step : (s + 1) * step
            ]


def table_from(got, rows, table, table2):
    peers, _, capacity = got.shape
    for h in range(peers * capacity // CHUNK):
        step = min(capacity, CHUNK)
        parts = []
        for s in range(CHUNK // step):
            lane = h * CHUNK + s * step
            peer, off = lane // capacity, lane % capacity
            parts.append(got[peer, :rows, off : off + step])
        value = parts[0] if len(parts) == 1 else jnp.concatenate(parts, axis=1)
        table[h * rows : (h + 1) * rows, :] = value
    table2[...] = split_wide(table[...])


def gather_elems(table2, pos_hi, hot_el, rows, visit):
    groups = table2.shape[0] // rows

    def body(i, _):
        at = pl.ds(pl.multiple_of(i * WIDE, WIDE), WIDE)
        visit(i, gather_cols(table2[...], pos_hi[:, at], hot_el[:, at], groups, rows))
        return 0

    lax.fori_loop(0, pos_hi.shape[1] // WIDE, body, 0)


def home_index(slot_row):
    slot = slot_row.astype(jnp.int32) - 1
    return jnp.where(slot < 0, -1, slot // CHUNK), jnp.maximum(slot, 0) % CHUNK


def apply_operator(x_all, ws, wm, coef_q, rhs, terms):
    rows = 3 * rhs
    stiff = dot3(x_all[...], ws[0], ws[1])
    mass = dot3(x_all[...], wm[0], wm[1])
    tensor = ((1, 4, 5), (4, 2, 6), (5, 6, 3))
    for i in range(x_all.shape[0] // rows):
        lanes = slice(i * CHUNK, (i + 1) * CHUNK)
        coef = coef_q[:, lanes]
        for c in range(3):
            at = i * rows + c * rhs
            total = coef[0:1] * stiff[at : at + rhs]
            for c2 in range(3):
                t = tensor[c][c2]
                at2 = i * rows + c2 * rhs
                total = total + coef[t : t + 1] * mass[at2 : at2 + rhs]
            terms[c * rhs : (c + 1) * rhs, lanes] = total


def edge_scatter(ea, eb, emap_hi, hot_ed, rhs, acc):
    groups = acc.shape[0] // rhs
    a_chunks = ea.shape[0] // rhs * CHUNK // WIDE
    acc[...] = jnp.zeros_like(acc)

    def put(i, values):
        at = pl.ds(pl.multiple_of(i * WIDE, WIDE), WIDE)
        acc[...] += scatter_cols(values, emap_hi[:, at], hot_ed[:, at], groups)

    def body(i, _):
        parts = [ea[pl.ds(pl.multiple_of((2 * i + s) * rhs, rhs), rhs), :] for s in range(2)]
        put(i, jnp.concatenate(parts, axis=1))
        return 0

    lax.fori_loop(0, a_chunks, body, 0)
    for i in range(2):
        parts = [eb[(4 * i + s) * rhs : (4 * i + s + 1) * rhs, :] for s in range(4)]
        put(a_chunks + i, jnp.concatenate(parts, axis=1))


def kernel(
    grps, peers, home, e_groups,
    res, emap, local, owner, slot, coef, pi, stiff, mass,
    out,
    rim_in, rim_out, rim_back, aux_send, aux_recv, send, recv,
    hot_el, hot_ed, hot_home, emap_hi, pos_hi, home_hi, slot_buf, coef_q, diag_q,
    wa, wb, ws, wm, e_table, e_table2, xa, xb, x3a, x3b, ea, eb, terms,
    n_table, n_table2, x_all, acc, acc_d, h_table, h_table2, rhs_nodes, h_acc, floored, e_acc,
    rim_s, rim_r, aux_s, aux_r, x_s, x_r, back_s, back_r,
):
    grp, me = lax.axis_index("grp"), lax.axis_index("dev")
    rhs = res.shape[0] // 2
    rows = 3 * rhs
    edges = res.shape[1]
    width = rim_in.shape[2]
    first, keep, step = cheb_factors()
    up, down = me + 1, me + peers - 1
    after_id = (lax.rem(grp + up // peers, grps), lax.rem(up, peers))
    before_id = (lax.rem(grp + grps - 1 + down // peers, grps), lax.rem(down, peers))

    def remote(src, dst, ssem, rsem, device):
        return pltpu.make_async_remote_copy(
            src_ref=src,
            dst_ref=dst,
            send_sem=ssem,
            recv_sem=rsem,
            device_id=device,
            device_id_type=pl.DeviceIdType.MESH,
        )

    def to_peer(src, dst, ssem, rsem, d):
        peer = lax.rem(me + d, peers)
        return remote(src.at[peer], dst.at[me], ssem.at[d], rsem.at[me], (grp, peer))

    def each_peer(do):
        def body(d, _):
            do(d)
            return 0

        lax.fori_loop(1, peers, body, 0)

    def wait_from(src, dst, ssem, rsem, s):
        remote(src.at[s], dst.at[s], ssem.at[0], rsem.at[s], (grp, s)).wait_recv()

    def source(d):
        return lax.rem(me + peers - d, peers)

    def refs(stage, half):
        return (send.at[stage, half], recv.at[stage, half], x_s.at[stage, half], x_r.at[stage, half])

    barrier = pltpu.get_barrier_semaphore()

    def greet(d):
        pl.semaphore_signal(
            barrier, 1, device_id=(grp, lax.rem(me + d, peers)),
            device_id_type=pl.DeviceIdType.MESH,
        )

    each_peer(greet)
    for device in (before_id, after_id):
        pl.semaphore_signal(barrier, 1, device_id=device, device_id_type=pl.DeviceIdType.MESH)
    pl.semaphore_wait(barrier, peers + 1)

    rims = [
        remote(res.at[:, edges - width :], rim_in.at[0], rim_s.at[0], rim_r.at[0], after_id),
        remote(res.at[:, :width], rim_in.at[1], rim_s.at[1], rim_r.at[1], before_id),
    ]
    for copy in rims:
        copy.start()

    prepare_places(peers, owner, slot, local, pos_hi, hot_el, slot_buf)
    prepare_coefs(coef, stiff, mass, coef_q, diag_q)
    scatter_elems(diag_q, pos_hi, hot_el, acc_d)
    for g in range(slot_buf.shape[0]):
        acc_d[g * AUX + 3 : g * AUX + 4, :] = slot_buf[g : g + 1, :]
    lay_out(aux_send, acc_d, AUX, 0)
    each_peer(lambda d: to_peer(aux_send, aux_recv, aux_s, aux_r, d).start())

    keep_parts(wa, pi_weights(pi[:128], 2, stiff.shape[0]))
    keep_parts(wb, pi_weights(pi[128:], 8, stiff.shape[0]))
    index = emap[...]
    emap_hi[...] = index // CHUNK

    def hot_edges(i, _):
        at = pl.ds(pl.multiple_of(i * WIDE, WIDE), WIDE)
        hot_ed[:, at] = onehot(emap[:, at] % CHUNK)
        return 0

    lax.fori_loop(0, emap.shape[1] // WIDE, hot_edges, 0)
    for copy in rims:
        copy.wait_recv()

    def restrict_half(half):
        mine = slice(half * rhs, (half + 1) * rhs)
        e_table[...] = jnp.zeros_like(e_table)
        blocks = [res[mine, i * CHUNK : (i + 1) * CHUNK] for i in range(edges // CHUNK)]
        for side in range(2):
            for i in range(width // CHUNK):
                blocks.append(rim_in[side, mine, i * CHUNK : (i + 1) * CHUNK])
        for h, block in enumerate(blocks):
            e_table[h * rhs : (h + 1) * rhs, :] = block
        e_table2[...] = split_wide(e_table[...])
        edge_gather(e_table2, emap_hi, hot_ed, e_groups, rhs, xa, xb)
        restrict(xa, xb, wa, wb, rhs, terms)
        scatter_elems(terms, pos_hi, hot_el, acc)
        lay_out(send.at[0, half], acc, rows, 0)
        each_peer(lambda d: to_peer(*refs(0, half), d).start())

    def learn_home():
        floored[...] = jnp.zeros_like(floored)

        def learn(got, s):
            high, low = home_index(got[s, 3:4, :])
            hot = onehot(low)
            home_hi[s] = high
            hot_home[s] = hot
            floored[...] += scatter_cols(got[s], high, hot, home)

        def other(d):
            s = source(d)
            wait_from(aux_send, aux_recv, aux_s, aux_r, s)
            learn(aux_recv, s)

        learn(aux_send, me)
        each_peer(other)
        floored[...] = jnp.maximum(floored[...], 1.0)

    def home_sum(stage, half, total):
        src, dst, ssem, rsem = refs(stage, half)
        total[...] = scatter_cols(src[me], home_hi[me], hot_home[me], home)

        def other(d):
            s = source(d)
            wait_from(src, dst, ssem, rsem, s)
            total[...] += scatter_cols(dst[s], home_hi[s], hot_home[s], home)

        each_peer(other)

    def home_values(h, c, half, second):
        at = slice(h * rows + c * rhs, h * rows + (c + 1) * rhs)
        weight = floored[h * AUX + c : h * AUX + c + 1, :]
        nodes = rhs_nodes[half, at, :]
        value = first * nodes / weight
        if second:
            value = keep * value + step * (nodes - h_acc[at, :]) / weight
        h_table[at, :] = value

    def home_half(stage, half, second):
        home_sum(stage, half, h_acc if second else rhs_nodes.at[half])
        h_table[...] = jnp.zeros_like(h_table)
        for h in range(home):
            for c in range(3):
                home_values(h, c, half, second)
        h_table2[...] = split_wide(h_table[...])
        src, dst, ssem, rsem = refs(stage + 1, half)

        def reply(d):
            peer = lax.rem(me + d, peers)
            src[peer] = gather_cols(h_table2[...], home_hi[peer], hot_home[peer], home, rows)
            to_peer(src, dst, ssem, rsem, d).start()

        each_peer(reply)
        dst[me] = gather_cols(h_table2[...], home_hi[me], hot_home[me], home, rows)

    def fetched(stage, half):
        each_peer(lambda d: wait_from(*refs(stage, half), source(d)))
        table_from(recv.at[stage, half], rows, n_table, n_table2)

    def operate_half(half):
        fetched(1, half)

        def visit(i, value):
            for s in range(2):
                at = pl.multiple_of((2 * i + s) * rows, rows)
                x_all[pl.ds(at, rows), :] = value[:, s * CHUNK : (s + 1) * CHUNK]

        gather_elems(n_table2, pos_hi, hot_el, rows, visit)
        apply_operator(x_all, ws, wm, coef_q, rhs, terms)
        scatter_elems(terms, pos_hi, hot_el, acc)
        lay_out(send.at[2, half], acc, rows, 0)
        each_peer(lambda d: to_peer(*refs(2, half), d).start())

    def backs(half):
        return [
            remote(
                rim_out.at[half, 0], rim_back.at[half, 1], back_s.at[half, 0],
                back_r.at[half, 0], before_id,
            ),
            remote(
                rim_out.at[half, 1], rim_back.at[half, 0], back_s.at[half, 1],
                back_r.at[half, 1], after_id,
            ),
        ]

    def prolong_half(half):
        fetched(3, half)

        def visit(i, value):
            for c in range(3):
                part = value[c * rhs : (c + 1) * rhs]
                x3b[pl.ds(pl.multiple_of(i * rhs, rhs), rhs), c * WIDE : (c + 1) * WIDE] = part
                for s in range(4):
                    at = pl.multiple_of((4 * i + s) * rhs, rhs)
                    x3a[pl.ds(at, rhs), c * 128 : (c + 1) * 128] = part[:, s * 128 : (s + 1) * 128]

        gather_elems(n_table2, pos_hi, hot_el, rows, visit)
        ea[...] = dot3_nt(x3a[...], wa[0], wa[1])
        eb[...] = dot3_nt(x3b[...], wb[0], wb[1])
        edge_scatter(ea, eb, emap_hi, hot_ed, rhs, e_acc.at[half])
        h = edges // CHUNK
        for side in range(2):
            for i in range(width // CHUNK):
                rim_out[half, side, :, i * CHUNK : (i + 1) * CHUNK] = e_acc[
                    half, h * rhs : (h + 1) * rhs, :
                ]
                h += 1
        for copy in backs(half):
            copy.start()

    restrict_half(0)
    learn_home()
    restrict_half(1)
    home_half(0, 0, False)
    keep_parts(ws, block_weights(stiff[...], 4))
    keep_parts(wm, block_weights(mass[...], 4))
    home_half(0, 1, False)
    operate_half(0)
    operate_half(1)
    home_half(2, 0, True)
    home_half(2, 1, True)
    prolong_half(0)
    prolong_half(1)

    count, reach = edges // CHUNK, width // CHUNK
    for half in range(2):
        mine = slice(half * rhs, (half + 1) * rhs)
        for copy in backs(half):
            copy.wait_recv()
        for h in range(count):
            value = e_acc[half, h * rhs : (h + 1) * rhs, :]
            if h < reach:
                value = value + rim_back[half, 0, :, h * CHUNK : (h + 1) * CHUNK]
            if h >= count - reach:
                at = (h - count + reach) * CHUNK
                value = value + rim_back[half, 1, :, at : at + CHUNK]
            out[mine, h * CHUNK : (h + 1) * CHUNK] = value

    for copy in rims + backs(0) + backs(1):
        copy.wait_send()

    def sent(d):
        to_peer(aux_send, aux_recv, aux_s, aux_r, d).wait_send()
        for stage in range(4):
            for half in range(2):
                to_peer(*refs(stage, half), d).wait_send()

    each_peer(sent)


def per_device(
    residual, pi, stiff, mass, permittivity, curl, edge_map, local_map, node_owner, node_slot
):
    rhs, edges = residual.shape
    ed, elems = edge_map.shape
    nodes = local_map.shape[0]
    touched = node_owner.shape[0]
    peers, grps = lax.axis_size("dev"), lax.axis_size("grp")
    capacity = 2 * touched // peers
    rim = edges // 8
    width = -(-rim // CHUNK) * CHUNK
    entries = nodes * elems
    place = edge_map.T - rim
    place = jnp.where(
        place < 0,
        place + edges + width,
        jnp.where(place >= edges, place + width, place),
    )
    emap = jnp.concatenate([place[:, :128].reshape(1, -1), place[:, 128:].reshape(1, -1)], axis=1)
    local = local_map.T.reshape(1, -1)
    coef = jnp.concatenate([curl[None], permittivity, jnp.zeros((1, elems), F32)], axis=0)
    groups = 2 * touched // CHUNK
    home = -(-N_LOC // CHUNK)
    home_even = home + home % 2
    e_groups = (edges + 2 * width) // CHUNK
    e_even = e_groups + e_groups % 2
    pairs, eights = elems // 2, elems // 8
    half = rhs // 2
    rows = 3 * half
    scratch = [
        ((2, rhs, width), F32),
        ((2, 2, half, width), F32),
        ((2, 2, half, width), F32),
        ((peers, AUX, capacity), F32),
        ((peers, AUX, capacity), F32),
        ((4, 2, peers, rows, capacity), F32),
        ((4, 2, peers, rows, capacity), F32),
        ((CHUNK, entries), BF16),
        ((CHUNK, ed * elems), BF16),
        ((peers, CHUNK, capacity), BF16),
        ((1, ed * elems), jnp.int32),
        ((1, entries), jnp.int32),
        ((peers, 1, capacity), jnp.int32),
        ((groups, CHUNK), F32),
        ((AUX, entries), F32),
        ((AUX, entries), F32),
        ((2, 256, 384), BF16),
        ((2, 128, 1536), BF16),
        ((2, CHUNK, CHUNK), BF16),
        ((2, CHUNK, CHUNK), BF16),
        ((e_even * half, CHUNK), F32),
        ((e_even * half, 2 * CHUNK), BF16),
        ((pairs * half, 256), F32),
        ((eights * half, 128), F32),
        ((pairs * half, 384), F32),
        ((eights * half, 1536), F32),
        ((pairs * half, 256), F32),
        ((eights * half, 128), F32),
        ((rows, entries), F32),
        ((groups * rows, CHUNK), F32),
        ((groups * rows, 2 * CHUNK), BF16),
        ((entries // CHUNK * rows, CHUNK), F32),
        ((groups * rows, CHUNK), F32),
        ((groups * AUX, CHUNK), F32),
        ((home_even * rows, CHUNK), F32),
        ((home_even * rows, 2 * CHUNK), BF16),
        ((2, home * rows, CHUNK), F32),
        ((home * rows, CHUNK), F32),
        ((home * AUX, CHUNK), F32),
        ((2, e_groups * half, CHUNK), F32),
    ]
    sems = [(2,), (2,), (peers,), (peers,), (4, 2, peers), (4, 2, peers), (2, 2), (2, 2)]
    vmem = pl.BlockSpec(memory_space=pltpu.VMEM)
    return pl.pallas_call(
        functools.partial(kernel, grps, peers, home, e_groups),
        out_shape=jax.ShapeDtypeStruct((rhs, edges), F32),
        in_specs=[vmem] * 9,
        out_specs=vmem,
        scratch_shapes=[pltpu.VMEM(*s) for s in scratch]
        + [pltpu.SemaphoreType.DMA(s) for s in sems],
        compiler_params=pltpu.CompilerParams(
            collective_id=0, has_side_effects=True, vmem_limit_bytes=VMEM_BYTES
        ),
    )(residual, emap, local, node_owner[None], node_slot[None], coef, pi, stiff, mass)


def solution(mesh):
    both = ("grp", "dev")
    in_specs = (
        P(None, both), P(), P(), P(), P(None, both), P(both), P(None, both), P(None, both),
        P(both), P(both),
    )
    return jax.shard_map(
        per_device, mesh=mesh, in_specs=in_specs, out_specs=P(None, both), check_vma=False
    )
```

```python
import functools
import jax
import jax.numpy as jnp
from jax import lax
from jax.experimental import pallas as pl
from jax.experimental.pallas import tpu as pltpu
from jax.sharding import PartitionSpec as P

N_LOC = 1728
CHUNK = 256
WIDE = 512
F32 = jnp.float32
BF16 = jnp.bfloat16
AUX = 8
CHEB_LOW = 0.3
CHEB_HIGH = 2.0
VMEM_BYTES = 60 * 1024 * 1024


def cheb_factors():
    center = 0.5 * (CHEB_HIGH + CHEB_LOW)
    half_width = 0.5 * (CHEB_HIGH - CHEB_LOW)
    sigma_ratio = center / half_width
    rho_first = 1.0 / sigma_ratio
    rho_second = 1.0 / (2.0 * sigma_ratio - rho_first)
    return (1.0 / center, 1.0 + rho_second * rho_first, 2.0 * rho_second / half_width)


def iota(shape, dim):
    return lax.broadcasted_iota(jnp.int32, shape, dim)


def dot(a, b):
    return lax.dot_general(a, b, (((1,), (0,)), ((), ())), preferred_element_type=F32)


def dot_nt(a, b):
    return lax.dot_general(a, b, (((1,), (1,)), ((), ())), preferred_element_type=F32)


def split(x):
    high = x.astype(BF16)
    low = (x - high.astype(F32)).astype(BF16)
    return high, low


def split_wide(x):
    high, low = split(x)
    return jnp.concatenate([high, low], axis=1)


def ones_where(mask):
    return jnp.where(mask, 1.0, 0.0).astype(BF16)


def onehot(low_index):
    return ones_where(iota((CHUNK, low_index.shape[1]), 0) == low_index)


def gather_cols(table2, high_index, hot, groups, rows):
    found = dot(table2, jnp.concatenate([hot, hot], axis=0))
    picked = jnp.zeros((rows, hot.shape[1]), F32)
    for h in range(groups):
        picked = jnp.where(high_index == h, found[h * rows : (h + 1) * rows], picked)
    return picked


def scatter_cols(values, high_index, hot, groups):
    count = 2 * values.shape[0] // 16
    high = values.astype(BF16).astype(F32)
    both = jnp.concatenate([high, values - high], axis=0).astype(BF16)
    index = jnp.concatenate([high_index] * count, axis=0) if count > 1 else high_index
    zero = jnp.zeros_like(both)
    spread = [jnp.where(index == jnp.int16(h), both, zero) for h in range(groups)]
    return dot_nt(jnp.concatenate(spread, axis=0), hot)


def add_parts(acc, found, rows, fresh=False):
    for h in range(found.shape[0] // (2 * rows)):
        at = slice(h * rows, (h + 1) * rows)
        low = 2 * h * rows
        value = found[low : low + rows] + found[low + rows : low + 2 * rows]
        acc[at, :] = value if fresh else acc[at, :] + value


def wide16(index):
    return jnp.broadcast_to(index, (16, index.shape[1])).astype(jnp.int16)


def dot3(x, w_high, w_low):
    high, low = split(x)
    return dot(high, w_high) + dot(low, w_high) + dot(high, w_low)


def dot3_nt(x, w_high, w_low):
    high, low = split(x)
    return dot_nt(high, w_high) + dot_nt(low, w_high) + dot_nt(high, w_low)


def block_weights(block, copies):
    size = block.shape[0]
    total = size * copies
    spread = ones_where(iota((size, total), 1) % size == iota((size, total), 0))
    keep = iota((total, total), 0) // size == iota((total, total), 1) // size
    out = []
    for part in split(block):
        row = dot(part, spread)
        full = jnp.concatenate([row] * copies, axis=0)
        out.append(jnp.where(keep, full, 0.0).astype(BF16))
    return out


def pi_weights(pi_rows, copies, nodes):
    count, total = pi_rows.shape
    comps = total // nodes
    width = comps * copies * nodes
    col, row = iota((total, width), 1), iota((total, width), 0)
    per = copies * nodes
    spread = ones_where((col // per == row // nodes) & (col % nodes == row % nodes))
    shape = (copies * count, width)
    keep = iota(shape, 0) // count == (iota(shape, 1) % per) // nodes
    out = []
    for part in split(pi_rows):
        one = dot(part, spread)
        full = jnp.concatenate([one] * copies, axis=0)
        out.append(jnp.where(keep, full, 0.0).astype(BF16))
    return out


def keep_parts(ref, parts):
    ref[0] = parts[0]
    ref[1] = parts[1]


def prepare_coefs(coef_ref, stiff_ref, mass_ref, coef_q, diag_q):
    nodes = stiff_ref.shape[0]
    eye = iota((nodes, nodes), 0) == iota((nodes, nodes), 1)
    sd = jnp.sum(jnp.where(eye, stiff_ref[...], 0.0), axis=0, keepdims=True)
    md = jnp.sum(jnp.where(eye, mass_ref[...], 0.0), axis=0, keepdims=True)
    diags = jnp.concatenate([sd, md, jnp.zeros((6, nodes), F32)], axis=0)
    d_parts = split(diags)
    c_parts = split(coef_ref[...])
    elems = coef_ref.shape[1]

    def body(i, _):
        lane = iota((elems, WIDE), 1) + i * WIDE
        by_elem = ones_where(lane // nodes == iota((elems, WIDE), 0))
        lane_n = iota((nodes, WIDE), 1)
        by_node = ones_where(lane_n % nodes == iota((nodes, WIDE), 0))
        coef = dot(c_parts[0], by_elem) + dot(c_parts[1], by_elem)
        diag = dot(d_parts[0], by_node) + dot(d_parts[1], by_node)
        at = pl.ds(pl.multiple_of(i * WIDE, WIDE), WIDE)
        coef_q[:, at] = coef
        base = coef[0:1] * diag[0:1]
        rows = iota((AUX, WIDE), 0)
        terms = jnp.zeros((AUX, WIDE), F32)
        for c in range(3):
            terms = jnp.where(rows == c, base + diag[1:2] * coef[1 + c : 2 + c], terms)
        diag_q[:, at] = terms
        return 0

    lax.fori_loop(0, coef_q.shape[1] // WIDE, body, 0)


def prepare_places(peers, owner_ref, slot_ref, local_ref, pos_hi, pos_hi16, hot_el, slot_buf):
    touched = owner_ref.shape[1]
    capacity = 2 * touched // peers
    groups = 2 * touched // CHUNK
    tri = ones_where(iota((CHUNK, CHUNK), 0) < iota((CHUNK, CHUNK), 1))
    carry = jnp.zeros((peers, 1), F32)
    place = []
    for i in range(touched // CHUNK):
        own = owner_ref[:, i * CHUNK : (i + 1) * CHUNK]
        hot = jnp.where(iota((peers, CHUNK), 0) == own, 1.0, 0.0)
        before = dot(hot.astype(BF16), tri) + carry
        rank = jnp.sum(hot * before, axis=0, keepdims=True)
        carry = carry + jnp.sum(hot, axis=1, keepdims=True)
        place.append(own * capacity + rank.astype(jnp.int32))
    rows8 = iota((AUX, CHUNK), 0)
    table_hi = jnp.zeros((AUX, CHUNK), F32)
    table_lo = jnp.zeros((AUX, CHUNK), F32)
    slots = jnp.zeros((2 * groups, CHUNK), F32)
    for i, pos in enumerate(place):
        high, low = pos // CHUNK, pos % CHUNK
        table_hi = jnp.where(rows8 == i, high.astype(F32), table_hi)
        table_lo = jnp.where(rows8 == i, low.astype(F32), table_lo)
        slot = slot_ref[:, i * CHUNK : (i + 1) * CHUNK] + 1
        here = iota((groups, CHUNK), 0) == high
        s_hi = jnp.where(here, (slot // CHUNK).astype(F32), 0.0)
        s_lo = jnp.where(here, (slot % CHUNK).astype(F32), 0.0)
        both = jnp.concatenate([s_hi, s_lo], axis=0).astype(BF16)
        slots = slots + dot_nt(both, onehot(low))
    slot_buf[...] = slots[:groups] * float(CHUNK) + slots[groups:]
    table = jnp.concatenate([table_hi, table_lo], axis=0).astype(BF16)

    def body(i, _):
        at = pl.ds(pl.multiple_of(i * WIDE, WIDE), WIDE)
        local = local_ref[:, at]
        found = dot(table, onehot(local % CHUNK))
        here = iota((AUX, WIDE), 0) == local // CHUNK
        high = jnp.sum(jnp.where(here, found[:AUX], 0.0), axis=0, keepdims=True)
        low = jnp.sum(jnp.where(here, found[AUX:], 0.0), axis=0, keepdims=True)
        pos_hi[:, at] = high.astype(jnp.int32)
        pos_hi16[:, at] = wide16(high.astype(jnp.int32))
        hot_el[:, at] = onehot(low.astype(jnp.int32))
        return 0

    lax.fori_loop(0, local_ref.shape[1] // WIDE, body, 0)


def edge_gather(table2, emap_hi, hot_ed, groups, rhs, xa, xb):
    a_chunks = xa.shape[0] // rhs * CHUNK // WIDE

    def take(i):
        at = pl.ds(pl.multiple_of(i * WIDE, WIDE), WIDE)
        return gather_cols(table2[...], emap_hi[:, at], hot_ed[:, at], groups, rhs)

    def body(i, _):
        got = take(i)
        for s in range(2):
            at = pl.multiple_of((2 * i + s) * rhs, rhs)
            xa[pl.ds(at, rhs), :] = got[:, s * CHUNK : (s + 1) * CHUNK]
        return 0

    lax.fori_loop(0, a_chunks, body, 0)
    for i in range(2):
        got = take(a_chunks + i)
        for s in range(4):
            xb[(4 * i + s) * rhs : (4 * i + s + 1) * rhs, :] = got[:, s * 128 : (s + 1) * 128]


def restrict(xa, xb, wa, wb, rhs, terms):
    ya = dot3(xa[...], wa[0], wa[1])
    yb = dot3(xb[...], wb[0], wb[1])
    for p in range(xa.shape[0] // rhs):
        for c in range(3):
            first = ya[p * rhs : (p + 1) * rhs, c * 128 : (c + 1) * 128]
            lane = c * 512 + (p % 4) * 128
            second = yb[(p // 4) * rhs : (p // 4 + 1) * rhs, lane : lane + 128]
            terms[c * rhs : (c + 1) * rhs, p * 128 : (p + 1) * 128] = first + second


def scatter_elems(terms, pos_hi16, hot_el, acc):
    rows, total = terms.shape
    groups = acc.shape[0] // rows
    acc[...] = jnp.zeros_like(acc)

    def body(i, _):
        at = pl.ds(pl.multiple_of(i * WIDE, WIDE), WIDE)
        add_parts(acc, scatter_cols(terms[:, at], pos_hi16[:, at], hot_el[:, at], groups), rows)
        return 0

    lax.fori_loop(0, total // WIDE, body, 0)


def lay_out(send, acc, rows):
    _, kept, capacity = send.shape
    for h in range(acc.shape[0] // rows):
        step = min(capacity, CHUNK)
        for s in range(CHUNK // step):
            lane = h * CHUNK + s * step
            peer, off = lane // capacity, lane % capacity
            send[peer, :, off : off + step] = acc[
                h * rows : h * rows + kept, s * step : (s + 1) * step
            ]


def table_from(got, rows, table, table2):
    peers, _, capacity = got.shape
    for h in range(peers * capacity // CHUNK):
        step = min(capacity, CHUNK)
        parts = []
        for s in range(CHUNK // step):
            lane = h * CHUNK + s * step
            peer, off = lane // capacity, lane % capacity
            parts.append(got[peer, :rows, off : off + step])
        value = parts[0] if len(parts) == 1 else jnp.concatenate(parts, axis=1)
        table[h * rows : (h + 1) * rows, :] = value
    table2[...] = split_wide(table[...])


def gather_elems(table2, pos_hi, hot_el, rows, visit):
    groups = table2.shape[0] // rows

    def body(i, _):
        at = pl.ds(pl.multiple_of(i * WIDE, WIDE), WIDE)
        visit(i, gather_cols(table2[...], pos_hi[:, at], hot_el[:, at], groups, rows))
        return 0

    lax.fori_loop(0, pos_hi.shape[1] // WIDE, body, 0)


def home_index(slot_row):
    slot = slot_row.astype(jnp.int32) - 1
    return jnp.where(slot < 0, -1, slot // CHUNK), jnp.maximum(slot, 0) % CHUNK


def apply_operator(x_all, ws, wm, coef_q, rhs, terms):
    rows = 3 * rhs
    stiff = dot3(x_all[...], ws[0], ws[1])
    mass = dot3(x_all[...], wm[0], wm[1])
    tensor = ((1, 4, 5), (4, 2, 6), (5, 6, 3))
    for i in range(x_all.shape[0] // rows):
        lanes = slice(i * CHUNK, (i + 1) * CHUNK)
        coef = coef_q[:, lanes]
        for c in range(3):
            at = i * rows + c * rhs
            total = coef[0:1] * stiff[at : at + rhs]
            for c2 in range(3):
                t = tensor[c][c2]
                at2 = i * rows + c2 * rhs
                total = total + coef[t : t + 1] * mass[at2 : at2 + rhs]
            terms[c * rhs : (c + 1) * rhs, lanes] = total


def edge_scatter(ea, eb, emap_hi16, hot_ed, rhs, acc):
    groups = acc.shape[0] // rhs
    a_chunks = ea.shape[0] // rhs * CHUNK // WIDE
    acc[...] = jnp.zeros_like(acc)

    def put(i, values):
        at = pl.ds(pl.multiple_of(i * WIDE, WIDE), WIDE)
        add_parts(acc, scatter_cols(values, emap_hi16[:, at], hot_ed[:, at], groups), rhs)

    def body(i, _):
        parts = [ea[pl.ds(pl.multiple_of((2 * i + s) * rhs, rhs), rhs), :] for s in range(2)]
        put(i, jnp.concatenate(parts, axis=1))
        return 0

    lax.fori_loop(0, a_chunks, body, 0)
    for i in range(2):
        parts = [eb[(4 * i + s) * rhs : (4 * i + s + 1) * rhs, :] for s in range(4)]
        put(a_chunks + i, jnp.concatenate(parts, axis=1))


def kernel(
    grps, peers, home, e_groups,
    res_in, emap, local, owner_in, slot_in, coef, pi_in, stiff_in, mass_in,
    out,
    res, owner, slot, pi, stiff, mass,
    rim_in, rim_out, rim_back, aux_send, aux_recv, send, recv,
    hot_el, hot_ed, hot_home, emap_hi, pos_hi, home_hi,
    emap_hi16, pos_hi16, home_hi16, slot_buf, coef_q, diag_q,
    wa, wb, ws, wm, e_table, e_table2, xa, xb, x3a, x3b, ea, eb, terms,
    n_table, n_table2, x_all, acc, acc_d, h_table, h_table2, rhs_nodes, h_acc, floored, e_acc,
    rim_s, rim_r, aux_s, aux_r, x_s, x_r, back_s, back_r, in_s,
):
    grp, me = lax.axis_index("grp"), lax.axis_index("dev")
    rhs = res.shape[0] // 2
    rows = 3 * rhs
    edges = res.shape[1]
    width = rim_in.shape[2]
    first, keep, step = cheb_factors()
    up, down = me + 1, me + peers - 1
    after_id = (lax.rem(grp + up // peers, grps), lax.rem(up, peers))
    before_id = (lax.rem(grp + grps - 1 + down // peers, grps), lax.rem(down, peers))

    def remote(src, dst, ssem, rsem, device):
        return pltpu.make_async_remote_copy(
            src_ref=src,
            dst_ref=dst,
            send_sem=ssem,
            recv_sem=rsem,
            device_id=device,
            device_id_type=pl.DeviceIdType.MESH,
        )

    def partner(m):
        total, bit = me * 0, 1
        while bit < peers:
            total = total + bit * lax.rem(me // bit + m // bit, 2)
            bit *= 2
        return total

    def to_peer(src, dst, ssem, rsem, m):
        peer = partner(m)
        return remote(src.at[peer], dst.at[me], ssem.at[m], rsem.at[m], (grp, peer))

    def each_peer(do):
        def body(i, _):
            do(peers - 1 - i)
            return 0

        lax.fori_loop(0, peers - 1, body, 0)

    def wait_from(src, dst, ssem, rsem, m):
        s = partner(m)
        remote(src.at[s], dst.at[s], ssem.at[m], rsem.at[m], (grp, s)).wait_recv()
        return s

    def refs(stage, half):
        return (send.at[stage, half], recv.at[stage, half], x_s.at[stage, half], x_r.at[stage, half])

    loads = [
        pltpu.make_async_copy(*pair, in_s.at[i])
        for i, pair in enumerate(
            [(owner_in, owner), (slot_in, slot), (pi_in, pi), (res_in, res), (stiff_in, stiff),
             (mass_in, mass)]
        )
    ]
    for load in loads:
        load.start()
    barrier = pltpu.get_barrier_semaphore()

    def greet(d):
        pl.semaphore_signal(
            barrier, 1, device_id=(grp, partner(d)),
            device_id_type=pl.DeviceIdType.MESH,
        )

    each_peer(greet)
    for device in (before_id, after_id):
        pl.semaphore_signal(barrier, 1, device_id=device, device_id_type=pl.DeviceIdType.MESH)
    pl.semaphore_wait(barrier, peers + 1)

    rims = [
        remote(res_in.at[:, edges - width :], rim_in.at[0], rim_s.at[0], rim_r.at[0], after_id),
        remote(res_in.at[:, :width], rim_in.at[1], rim_s.at[1], rim_r.at[1], before_id),
    ]
    for copy in rims:
        copy.start()

    loads[0].wait()
    loads[1].wait()
    prepare_places(peers, owner, slot, local, pos_hi, pos_hi16, hot_el, slot_buf)
    loads[2].wait()
    nodes = stiff.shape[0]
    keep_parts(wa, pi_weights(pi[:128], 2, nodes))
    keep_parts(wb, pi_weights(pi[128:], 8, nodes))

    def hot_edges(i, _):
        at = pl.ds(pl.multiple_of(i * WIDE, WIDE), WIDE)
        index = emap[:, at]
        emap_hi[:, at] = index // CHUNK
        emap_hi16[:, at] = wide16(index // CHUNK)
        hot_ed[:, at] = onehot(index % CHUNK)
        return 0

    lax.fori_loop(0, emap.shape[1] // WIDE, hot_edges, 0)
    loads[3].wait()
    for copy in rims:
        copy.wait_recv()

    def send_aux():
        loads[4].wait()
        loads[5].wait()
        prepare_coefs(coef, stiff, mass, coef_q, diag_q)
        scatter_elems(diag_q, pos_hi16, hot_el, acc_d)
        for g in range(slot_buf.shape[0]):
            acc_d[g * AUX + 3 : g * AUX + 4, :] = slot_buf[g : g + 1, :]
        lay_out(aux_send, acc_d, AUX)
        each_peer(lambda d: to_peer(aux_send, aux_recv, aux_s, aux_r, d).start())

    def restrict_half(half):
        mine = slice(half * rhs, (half + 1) * rhs)
        e_table[...] = jnp.zeros_like(e_table)
        blocks = [res[mine, i * CHUNK : (i + 1) * CHUNK] for i in range(edges // CHUNK)]
        for side in range(2):
            for i in range(width // CHUNK):
                blocks.append(rim_in[side, mine, i * CHUNK : (i + 1) * CHUNK])
        for h, block in enumerate(blocks):
            e_table[h * rhs : (h + 1) * rhs, :] = block
        e_table2[...] = split_wide(e_table[...])
        edge_gather(e_table2, emap_hi, hot_ed, e_groups, rhs, xa, xb)
        restrict(xa, xb, wa, wb, rhs, terms)
        scatter_elems(terms, pos_hi16, hot_el, acc)
        lay_out(send.at[0, half], acc, rows)
        each_peer(lambda d: to_peer(*refs(0, half), d).start())

    def learn_home():
        floored[...] = jnp.zeros_like(floored)

        def learn(got, s):
            high, low = home_index(got[s, 3:4, :])
            hot = onehot(low)
            home_hi[s] = high
            hot_home[s] = hot
            high16 = wide16(high)
            home_hi16[s] = high16
            values = jnp.concatenate([got[s], jnp.zeros_like(got[s])], axis=0)
            add_parts(floored, scatter_cols(values, high16, hot, home), AUX)

        def other(d):
            learn(aux_recv, wait_from(aux_send, aux_recv, aux_s, aux_r, d))

        learn(aux_send, me)
        each_peer(other)
        floored[...] = jnp.maximum(floored[...], 1.0)

    def home_sum(stage, half, total):
        src, dst, ssem, rsem = refs(stage, half)
        add_parts(total, scatter_cols(src[me], home_hi16[me], hot_home[me], home), rows, True)

        def other(d):
            s = wait_from(src, dst, ssem, rsem, d)
            add_parts(total, scatter_cols(dst[s], home_hi16[s], hot_home[s], home), rows)

        each_peer(other)

    def home_values(h, c, half, second):
        at = slice(h * rows + c * rhs, h * rows + (c + 1) * rhs)
        weight = floored[h * AUX + c : h * AUX + c + 1, :]
        nodes = rhs_nodes[half, at, :]
        value = first * nodes / weight
        if second:
            value = keep * value + step * (nodes - h_acc[at, :]) / weight
        h_table[at, :] = value

    def home_half(stage, half, second):
        home_sum(stage, half, h_acc if second else rhs_nodes.at[half])
        h_table[...] = jnp.zeros_like(h_table)
        for h in range(home):
            for c in range(3):
                home_values(h, c, half, second)
        h_table2[...] = split_wide(h_table[...])
        src, dst, ssem, rsem = refs(stage + 1, half)

        def reply(d):
            peer = partner(d)
            src[peer] = gather_cols(h_table2[...], home_hi[peer], hot_home[peer], home, rows)
            to_peer(src, dst, ssem, rsem, d).start()

        each_peer(reply)
        dst[me] = gather_cols(h_table2[...], home_hi[me], hot_home[me], home, rows)

    def fetched(stage, half):
        each_peer(lambda d: wait_from(*refs(stage, half), d))
        table_from(recv.at[stage, half], rows, n_table, n_table2)

    def operate_half(half):
        fetched(1, half)

        def visit(i, value):
            for s in range(2):
                at = pl.multiple_of((2 * i + s) * rows, rows)
                x_all[pl.ds(at, rows), :] = value[:, s * CHUNK : (s + 1) * CHUNK]

        gather_elems(n_table2, pos_hi, hot_el, rows, visit)
        apply_operator(x_all, ws, wm, coef_q, rhs, terms)
        scatter_elems(terms, pos_hi16, hot_el, acc)
        lay_out(send.at[2, half], acc, rows)
        each_peer(lambda d: to_peer(*refs(2, half), d).start())

    def backs(half):
        return [
            remote(
                rim_out.at[half, 0], rim_back.at[half, 1], back_s.at[half, 0],
                back_r.at[half, 0], before_id,
            ),
            remote(
                rim_out.at[half, 1], rim_back.at[half, 0], back_s.at[half, 1],
                back_r.at[half, 1], after_id,
            ),
        ]

    def prolong_half(half):
        fetched(3, half)

        def visit(i, value):
            for c in range(3):
                part = value[c * rhs : (c + 1) * rhs]
                x3b[pl.ds(pl.multiple_of(i * rhs, rhs), rhs), c * WIDE : (c + 1) * WIDE] = part
                for s in range(4):
                    at = pl.multiple_of((4 * i + s) * rhs, rhs)
                    x3a[pl.ds(at, rhs), c * 128 : (c + 1) * 128] = part[:, s * 128 : (s + 1) * 128]

        gather_elems(n_table2, pos_hi, hot_el, rows, visit)
        ea[...] = dot3_nt(x3a[...], wa[0], wa[1])
        eb[...] = dot3_nt(x3b[...], wb[0], wb[1])
        edge_scatter(ea, eb, emap_hi16, hot_ed, rhs, e_acc.at[half])
        h = edges // CHUNK
        for side in range(2):
            for i in range(width // CHUNK):
                rim_out[half, side, :, i * CHUNK : (i + 1) * CHUNK] = e_acc[
                    half, h * rhs : (h + 1) * rhs, :
                ]
                h += 1
        for copy in backs(half):
            copy.start()

    restrict_half(0)
    send_aux()
    restrict_half(1)
    keep_parts(ws, block_weights(stiff[...], 4))
    keep_parts(wm, block_weights(mass[...], 4))
    learn_home()
    home_half(0, 0, False)
    home_half(0, 1, False)
    operate_half(0)
    operate_half(1)
    home_half(2, 0, True)
    home_half(2, 1, True)
    prolong_half(0)
    prolong_half(1)

    count, reach = edges // CHUNK, width // CHUNK
    for half in range(2):
        mine = slice(half * rhs, (half + 1) * rhs)
        for copy in backs(half):
            copy.wait_recv()
        for h in range(count):
            value = e_acc[half, h * rhs : (h + 1) * rhs, :]
            if h < reach:
                value = value + rim_back[half, 0, :, h * CHUNK : (h + 1) * CHUNK]
            if h >= count - reach:
                at = (h - count + reach) * CHUNK
                value = value + rim_back[half, 1, :, at : at + CHUNK]
            out[mine, h * CHUNK : (h + 1) * CHUNK] = value

    for copy in rims + backs(0) + backs(1):
        copy.wait_send()

    def sent(d):
        to_peer(aux_send, aux_recv, aux_s, aux_r, d).wait_send()
        for stage in range(4):
            for half in range(2):
                to_peer(*refs(stage, half), d).wait_send()

    each_peer(sent)


def per_device(
    residual, pi, stiff, mass, permittivity, curl, edge_map, local_map, node_owner, node_slot
):
    rhs, edges = residual.shape
    ed, elems = edge_map.shape
    nodes = local_map.shape[0]
    touched = node_owner.shape[0]
    peers, grps = lax.axis_size("dev"), lax.axis_size("grp")
    capacity = 2 * touched // peers
    rim = edges // 8
    width = -(-rim // CHUNK) * CHUNK
    entries = nodes * elems
    place = edge_map.T - rim
    place = jnp.where(
        place < 0,
        place + edges + width,
        jnp.where(place >= edges, place + width, place),
    )
    emap = jnp.concatenate([place[:, :128].reshape(1, -1), place[:, 128:].reshape(1, -1)], axis=1)
    local = local_map.T.reshape(1, -1)
    coef = jnp.concatenate([curl[None], permittivity, jnp.zeros((1, elems), F32)], axis=0)
    groups = 2 * touched // CHUNK
    home = -(-N_LOC // CHUNK)
    home_even = home + home % 2
    e_groups = (edges + 2 * width) // CHUNK
    e_even = e_groups + e_groups % 2
    pairs, eights = elems // 2, elems // 8
    half = rhs // 2
    rows = 3 * half
    scratch = [
        ((rhs, edges), F32),
        ((1, touched), jnp.int32),
        ((1, touched), jnp.int32),
        (pi.shape, F32),
        (stiff.shape, F32),
        (mass.shape, F32),
        ((2, rhs, width), F32),
        ((2, 2, half, width), F32),
        ((2, 2, half, width), F32),
        ((peers, AUX // 2, capacity), F32),
        ((peers, AUX // 2, capacity), F32),
        ((4, 2, peers, rows, capacity), F32),
        ((4, 2, peers, rows, capacity), F32),
        ((CHUNK, entries), BF16),
        ((CHUNK, ed * elems), BF16),
        ((peers, CHUNK, capacity), BF16),
        ((1, ed * elems), jnp.int32),
        ((1, entries), jnp.int32),
        ((peers, 1, capacity), jnp.int32),
        ((16, ed * elems), jnp.int16),
        ((16, entries), jnp.int16),
        ((peers, 16, capacity), jnp.int16),
        ((groups, CHUNK), F32),
        ((AUX, entries), F32),
        ((AUX, entries), F32),
        ((2, 256, 384), BF16),
        ((2, 128, 1536), BF16),
        ((2, CHUNK, CHUNK), BF16),
        ((2, CHUNK, CHUNK), BF16),
        ((e_even * half, CHUNK), F32),
        ((e_even * half, 2 * CHUNK), BF16),
        ((pairs * half, 256), F32),
        ((eights * half, 128), F32),
        ((pairs * half, 384), F32),
        ((eights * half, 1536), F32),
        ((pairs * half, 256), F32),
        ((eights * half, 128), F32),
        ((rows, entries), F32),
        ((groups * rows, CHUNK), F32),
        ((groups * rows, 2 * CHUNK), BF16),
        ((entries // CHUNK * rows, CHUNK), F32),
        ((groups * rows, CHUNK), F32),
        ((groups * AUX, CHUNK), F32),
        ((home_even * rows, CHUNK), F32),
        ((home_even * rows, 2 * CHUNK), BF16),
        ((2, home * rows, CHUNK), F32),
        ((home * rows, CHUNK), F32),
        ((home * AUX, CHUNK), F32),
        ((2, e_groups * half, CHUNK), F32),
    ]
    sems = [(2,), (2,), (peers,), (peers,), (4, 2, peers), (4, 2, peers), (2, 2), (2, 2), (6,)]
    vmem, where = pl.BlockSpec(memory_space=pltpu.VMEM), pl.BlockSpec(memory_space=pl.ANY)
    return pl.pallas_call(
        functools.partial(kernel, grps, peers, home, e_groups),
        out_shape=jax.ShapeDtypeStruct((rhs, edges), F32),
        in_specs=[where, vmem, vmem, where, where, vmem, where, where, where],
        out_specs=vmem,
        scratch_shapes=[pltpu.VMEM(*s) for s in scratch]
        + [pltpu.SemaphoreType.DMA(s) for s in sems],
        compiler_params=pltpu.CompilerParams(
            collective_id=0, has_side_effects=True, vmem_limit_bytes=VMEM_BYTES
        ),
    )(residual, emap, local, node_owner[None], node_slot[None], coef, pi, stiff, mass)


def solution(mesh):
    both = ("grp", "dev")
    in_specs = (
        P(None, both), P(), P(), P(), P(None, both), P(both), P(None, both), P(None, both),
        P(both), P(both),
    )
    return jax.shard_map(
        per_device, mesh=mesh, in_specs=in_specs, out_specs=P(None, both), check_vma=False
    )
```

```python
import functools
import math
import jax
import jax.numpy as jnp
from jax import lax
from jax.experimental import pallas as pl
from jax.experimental.pallas import tpu as pltpu
from jax.sharding import PartitionSpec as P

N_LOC = 1728
CHUNK = 256
WIDE = 512
F32 = jnp.float32
BF16 = jnp.bfloat16
AUX = 8
FULL = 4096.0
CHEB_LOW = 0.3
CHEB_HIGH = 2.0
VMEM_BYTES = 60 * 1024 * 1024


def cheb_factors():
    center = 0.5 * (CHEB_HIGH + CHEB_LOW)
    half_width = 0.5 * (CHEB_HIGH - CHEB_LOW)
    sigma_ratio = center / half_width
    rho_first = 1.0 / sigma_ratio
    rho_second = 1.0 / (2.0 * sigma_ratio - rho_first)
    return (1.0 / center, 1.0 + rho_second * rho_first, 2.0 * rho_second / half_width)


def iota(shape, dim):
    return lax.broadcasted_iota(jnp.int32, shape, dim)


def dot(a, b):
    return lax.dot_general(a, b, (((1,), (0,)), ((), ())), preferred_element_type=F32)


def dot_nt(a, b):
    return lax.dot_general(a, b, (((1,), (1,)), ((), ())), preferred_element_type=F32)


def split(x):
    high = x.astype(BF16)
    low = (x - high.astype(F32)).astype(BF16)
    return high, low


def split_wide(x):
    high, low = split(x)
    return jnp.concatenate([high, low], axis=1)


def ones_where(mask):
    return jnp.where(mask, 1.0, 0.0).astype(BF16)


def onehot(low_index):
    return ones_where(iota((CHUNK, low_index.shape[1]), 0) == low_index)


def gather_cols(table2, high_index, hot, groups, rows):
    found = dot(table2, jnp.concatenate([hot, hot], axis=0))
    picked = jnp.zeros((rows, hot.shape[1]), F32)
    for h in range(groups):
        picked = jnp.where(high_index == h, found[h * rows : (h + 1) * rows], picked)
    return picked


def scatter_cols(values, high_index, hot, groups):
    count = 2 * values.shape[0] // 16
    high = values.astype(BF16).astype(F32)
    both = jnp.concatenate([high, values - high], axis=0).astype(BF16)
    index = jnp.concatenate([high_index] * count, axis=0) if count > 1 else high_index
    zero = jnp.zeros_like(both)
    spread = [jnp.where(index == jnp.int16(h), both, zero) for h in range(groups)]
    return dot_nt(jnp.concatenate(spread, axis=0), hot)


def add_parts(acc, found, rows, fresh=False):
    for h in range(found.shape[0] // (2 * rows)):
        at = slice(h * rows, (h + 1) * rows)
        low = 2 * h * rows
        value = found[low : low + rows] + found[low + rows : low + 2 * rows]
        acc[at, :] = value if fresh else acc[at, :] + value


def wide16(index):
    return jnp.broadcast_to(index, (16, index.shape[1])).astype(jnp.int16)


def dot3(x, w_high, w_low):
    high, low = split(x)
    return dot(high, w_high) + dot(low, w_high) + dot(high, w_low)


def dot3_nt(x, w_high, w_low):
    high, low = split(x)
    return dot_nt(high, w_high) + dot_nt(low, w_high) + dot_nt(high, w_low)


def block_weights(block, copies):
    size = block.shape[0]
    total = size * copies
    spread = ones_where(iota((size, total), 1) % size == iota((size, total), 0))
    keep = iota((total, total), 0) // size == iota((total, total), 1) // size
    out = []
    for part in split(block):
        row = dot(part, spread)
        full = jnp.concatenate([row] * copies, axis=0)
        out.append(jnp.where(keep, full, 0.0).astype(BF16))
    return out


def pi_weights(pi_rows, copies, nodes):
    count, total = pi_rows.shape
    comps = total // nodes
    width = comps * copies * nodes
    col, row = iota((total, width), 1), iota((total, width), 0)
    per = copies * nodes
    spread = ones_where((col // per == row // nodes) & (col % nodes == row % nodes))
    shape = (copies * count, width)
    keep = iota(shape, 0) // count == (iota(shape, 1) % per) // nodes
    out = []
    for part in split(pi_rows):
        one = dot(part, spread)
        full = jnp.concatenate([one] * copies, axis=0)
        out.append(jnp.where(keep, full, 0.0).astype(BF16))
    return out


def keep_parts(ref, parts):
    ref[0] = parts[0]
    ref[1] = parts[1]


def prepare_coefs(coef_ref, stiff_ref, mass_ref, coef_q, diag_q):
    nodes = stiff_ref.shape[0]
    eye = iota((nodes, nodes), 0) == iota((nodes, nodes), 1)
    sd = jnp.sum(jnp.where(eye, stiff_ref[...], 0.0), axis=0, keepdims=True)
    md = jnp.sum(jnp.where(eye, mass_ref[...], 0.0), axis=0, keepdims=True)
    diags = jnp.concatenate([sd, md, jnp.zeros((6, nodes), F32)], axis=0)
    d_parts = split(diags)
    c_parts = split(coef_ref[...])
    elems = coef_ref.shape[1]

    def body(i, _):
        lane = iota((elems, WIDE), 1) + i * WIDE
        by_elem = ones_where(lane // nodes == iota((elems, WIDE), 0))
        lane_n = iota((nodes, WIDE), 1)
        by_node = ones_where(lane_n % nodes == iota((nodes, WIDE), 0))
        coef = dot(c_parts[0], by_elem) + dot(c_parts[1], by_elem)
        diag = dot(d_parts[0], by_node) + dot(d_parts[1], by_node)
        at = pl.ds(pl.multiple_of(i * WIDE, WIDE), WIDE)
        coef_q[:, at] = coef
        base = coef[0:1] * diag[0:1]
        rows = iota((AUX, WIDE), 0)
        terms = jnp.zeros((AUX, WIDE), F32)
        for c in range(3):
            terms = jnp.where(rows == c, base + diag[1:2] * coef[1 + c : 2 + c], terms)
        diag_q[:, at] = terms
        return 0

    lax.fori_loop(0, coef_q.shape[1] // WIDE, body, 0)


def prepare_places(peers, capacity, spread, owner_ref, slot_ref, local_ref, pos_hi, pos_hi16, hot_el, slot_buf):
    touched = owner_ref.shape[1]
    groups = slot_buf.shape[0]
    per = -(-N_LOC // peers)
    tri = ones_where(iota((CHUNK, CHUNK), 0) < iota((CHUNK, CHUNK), 1))
    carry = jnp.zeros((peers, 1), F32)
    place, kept = [], []
    for i in range(touched // CHUNK):
        own = owner_ref[:, i * CHUNK : (i + 1) * CHUNK]
        slot = slot_ref[:, i * CHUNK : (i + 1) * CHUNK]
        if spread:
            own, slot = slot % peers, own * per + slot // peers
        kept.append(slot + 1)
        hot = jnp.where(iota((peers, CHUNK), 0) == own, 1.0, 0.0)
        before = dot(hot.astype(BF16), tri) + carry
        rank = jnp.sum(hot * before, axis=0, keepdims=True)
        carry = carry + jnp.sum(hot, axis=1, keepdims=True)
        place.append(own * capacity + rank.astype(jnp.int32))
    rows8 = iota((AUX, CHUNK), 0)
    table_hi = jnp.zeros((AUX, CHUNK), F32)
    table_lo = jnp.zeros((AUX, CHUNK), F32)
    slots = jnp.zeros((2 * groups, CHUNK), F32)
    for i, pos in enumerate(place):
        high, low = pos // CHUNK, pos % CHUNK
        table_hi = jnp.where(rows8 == i, high.astype(F32), table_hi)
        table_lo = jnp.where(rows8 == i, low.astype(F32), table_lo)
        slot = kept[i]
        here = iota((groups, CHUNK), 0) == high
        s_hi = jnp.where(here, (slot // CHUNK).astype(F32), 0.0)
        s_lo = jnp.where(here, (slot % CHUNK).astype(F32), 0.0)
        both = jnp.concatenate([s_hi, s_lo], axis=0).astype(BF16)
        slots = slots + dot_nt(both, onehot(low))
    numbers = slots[:groups] * float(CHUNK) + slots[groups:]
    if spread:
        most = jnp.max(carry, axis=0, keepdims=True)
        numbers = numbers + jnp.where(most > float(capacity), FULL, 0.0)
    slot_buf[...] = numbers
    table = jnp.concatenate([table_hi, table_lo], axis=0).astype(BF16)

    def body(i, _):
        at = pl.ds(pl.multiple_of(i * WIDE, WIDE), WIDE)
        local = local_ref[:, at]
        found = dot(table, onehot(local % CHUNK))
        here = iota((AUX, WIDE), 0) == local // CHUNK
        high = jnp.sum(jnp.where(here, found[:AUX], 0.0), axis=0, keepdims=True)
        low = jnp.sum(jnp.where(here, found[AUX:], 0.0), axis=0, keepdims=True)
        pos_hi[:, at] = high.astype(jnp.int32)
        pos_hi16[:, at] = wide16(high.astype(jnp.int32))
        hot_el[:, at] = onehot(low.astype(jnp.int32))
        return 0

    lax.fori_loop(0, local_ref.shape[1] // WIDE, body, 0)


def edge_gather(table2, emap_hi, hot_ed, groups, rhs, xa, xb):
    a_chunks = xa.shape[0] // rhs * CHUNK // WIDE

    def take(i):
        at = pl.ds(pl.multiple_of(i * WIDE, WIDE), WIDE)
        return gather_cols(table2[...], emap_hi[:, at], hot_ed[:, at], groups, rhs)

    def body(i, _):
        got = take(i)
        for s in range(2):
            at = pl.multiple_of((2 * i + s) * rhs, rhs)
            xa[pl.ds(at, rhs), :] = got[:, s * CHUNK : (s + 1) * CHUNK]
        return 0

    lax.fori_loop(0, a_chunks, body, 0)
    for i in range(2):
        got = take(a_chunks + i)
        for s in range(4):
            xb[(4 * i + s) * rhs : (4 * i + s + 1) * rhs, :] = got[:, s * 128 : (s + 1) * 128]


def restrict(xa, xb, wa, wb, rhs, terms):
    ya = dot3(xa[...], wa[0], wa[1])
    yb = dot3(xb[...], wb[0], wb[1])
    for p in range(xa.shape[0] // rhs):
        for c in range(3):
            first = ya[p * rhs : (p + 1) * rhs, c * 128 : (c + 1) * 128]
            lane = c * 512 + (p % 4) * 128
            second = yb[(p // 4) * rhs : (p // 4 + 1) * rhs, lane : lane + 128]
            terms[c * rhs : (c + 1) * rhs, p * 128 : (p + 1) * 128] = first + second


def scatter_elems(terms, pos_hi16, hot_el, acc):
    rows, total = terms.shape
    groups = acc.shape[0] // rows
    acc[...] = jnp.zeros_like(acc)

    def body(i, _):
        at = pl.ds(pl.multiple_of(i * WIDE, WIDE), WIDE)
        add_parts(acc, scatter_cols(terms[:, at], pos_hi16[:, at], hot_el[:, at], groups), rows)
        return 0

    lax.fori_loop(0, total // WIDE, body, 0)


def lay_out(send, acc, rows):
    _, kept, capacity = send.shape
    for h in range(acc.shape[0] // rows):
        step = math.gcd(capacity, CHUNK)
        for s in range(CHUNK // step):
            lane = h * CHUNK + s * step
            peer, off = lane // capacity, lane % capacity
            send[peer, :, off : off + step] = acc[
                h * rows : h * rows + kept, s * step : (s + 1) * step
            ]


def table_from(got, rows, table, table2):
    peers, _, capacity = got.shape
    for h in range(peers * capacity // CHUNK):
        step = math.gcd(capacity, CHUNK)
        parts = []
        for s in range(CHUNK // step):
            lane = h * CHUNK + s * step
            peer, off = lane // capacity, lane % capacity
            parts.append(got[peer, :rows, off : off + step])
        value = parts[0] if len(parts) == 1 else jnp.concatenate(parts, axis=1)
        table[h * rows : (h + 1) * rows, :] = value
    table2[...] = split_wide(table[...])


def gather_elems(table2, pos_hi, hot_el, rows, visit):
    groups = table2.shape[0] // rows

    def body(i, _):
        at = pl.ds(pl.multiple_of(i * WIDE, WIDE), WIDE)
        visit(i, gather_cols(table2[...], pos_hi[:, at], hot_el[:, at], groups, rows))
        return 0

    lax.fori_loop(0, pos_hi.shape[1] // WIDE, body, 0)


def home_index(slot_row):
    slot = slot_row.astype(jnp.int32) - 1
    return jnp.where(slot < 0, -1, slot // CHUNK), jnp.maximum(slot, 0) % CHUNK


def apply_operator(x_all, ws, wm, coef_q, rhs, terms):
    rows = 3 * rhs
    stiff = dot3(x_all[...], ws[0], ws[1])
    mass = dot3(x_all[...], wm[0], wm[1])
    tensor = ((1, 4, 5), (4, 2, 6), (5, 6, 3))
    for i in range(x_all.shape[0] // rows):
        lanes = slice(i * CHUNK, (i + 1) * CHUNK)
        coef = coef_q[:, lanes]
        for c in range(3):
            at = i * rows + c * rhs
            total = coef[0:1] * stiff[at : at + rhs]
            for c2 in range(3):
                t = tensor[c][c2]
                at2 = i * rows + c2 * rhs
                total = total + coef[t : t + 1] * mass[at2 : at2 + rhs]
            terms[c * rhs : (c + 1) * rhs, lanes] = total


def edge_scatter(ea, eb, emap_hi16, hot_ed, rhs, acc):
    groups = acc.shape[0] // rhs
    a_chunks = ea.shape[0] // rhs * CHUNK // WIDE
    acc[...] = jnp.zeros_like(acc)

    def put(i, values):
        at = pl.ds(pl.multiple_of(i * WIDE, WIDE), WIDE)
        add_parts(acc, scatter_cols(values, emap_hi16[:, at], hot_ed[:, at], groups), rhs)

    def body(i, _):
        parts = [ea[pl.ds(pl.multiple_of((2 * i + s) * rhs, rhs), rhs), :] for s in range(2)]
        put(i, jnp.concatenate(parts, axis=1))
        return 0

    lax.fori_loop(0, a_chunks, body, 0)
    for i in range(2):
        parts = [eb[(4 * i + s) * rhs : (4 * i + s + 1) * rhs, :] for s in range(4)]
        put(a_chunks + i, jnp.concatenate(parts, axis=1))


def kernel(
    grps, peers, home, e_groups, capacity, spread,
    res_in, emap, local, owner_in, slot_in, coef, pi_in, stiff_in, mass_in,
    out, flag_out,
    res, owner, slot, pi, stiff, mass,
    rim_in, rim_out, rim_back, aux_send, aux_recv, send, recv,
    hot_el, hot_ed, hot_home, emap_hi, pos_hi, home_hi,
    emap_hi16, pos_hi16, home_hi16, slot_buf, coef_q, diag_q,
    wa, wb, ws, wm, e_table, e_table2, xa, xb, x3a, x3b, ea, eb, terms,
    n_table, n_table2, x_all, acc, acc_d, h_table, h_table2, rhs_nodes, h_acc, floored, e_acc, flag, flag_in,
    rim_s, rim_r, aux_s, aux_r, x_s, x_r, back_s, back_r, in_s, flag_s, flag_r,
):
    grp, me = lax.axis_index("grp"), lax.axis_index("dev")
    rhs = res.shape[0] // 2
    rows = 3 * rhs
    edges = res.shape[1]
    width = rim_in.shape[2]
    first, keep, step = cheb_factors()
    up, down = me + 1, me + peers - 1
    after_id = (lax.rem(grp + up // peers, grps), lax.rem(up, peers))
    before_id = (lax.rem(grp + grps - 1 + down // peers, grps), lax.rem(down, peers))

    def remote(src, dst, ssem, rsem, device):
        return pltpu.make_async_remote_copy(
            src_ref=src,
            dst_ref=dst,
            send_sem=ssem,
            recv_sem=rsem,
            device_id=device,
            device_id_type=pl.DeviceIdType.MESH,
        )

    def partner(m):
        total, bit = me * 0, 1
        while bit < peers:
            total = total + bit * lax.rem(me // bit + m // bit, 2)
            bit *= 2
        return total

    def to_peer(src, dst, ssem, rsem, m):
        peer = partner(m)
        return remote(src.at[peer], dst.at[me], ssem.at[m], rsem.at[m], (grp, peer))

    def each_peer(do):
        def body(i, _):
            do(peers - 1 - i)
            return 0

        lax.fori_loop(0, peers - 1, body, 0)

    def wait_from(src, dst, ssem, rsem, m):
        s = partner(m)
        remote(src.at[s], dst.at[s], ssem.at[m], rsem.at[m], (grp, s)).wait_recv()
        return s

    def refs(stage, half):
        return (send.at[stage, half], recv.at[stage, half], x_s.at[stage, half], x_r.at[stage, half])

    loads = [
        pltpu.make_async_copy(*pair, in_s.at[i])
        for i, pair in enumerate(
            [(owner_in, owner), (slot_in, slot), (pi_in, pi), (res_in, res), (stiff_in, stiff),
             (mass_in, mass)]
        )
    ]
    for load in loads:
        load.start()
    barrier = pltpu.get_barrier_semaphore()

    def greet(d):
        pl.semaphore_signal(
            barrier, 1, device_id=(grp, partner(d)),
            device_id_type=pl.DeviceIdType.MESH,
        )

    each_peer(greet)
    others = [(lax.rem(grp + d, grps), me) for d in range(1, grps)]
    for device in [before_id, after_id] + others:
        pl.semaphore_signal(barrier, 1, device_id=device, device_id_type=pl.DeviceIdType.MESH)
    pl.semaphore_wait(barrier, peers + grps)
    flags = [
        remote(flag, flag_in.at[i], flag_s.at[i], flag_r.at[i], device)
        for i, device in enumerate(others)
    ]

    rims = [
        remote(res_in.at[:, edges - width :], rim_in.at[0], rim_s.at[0], rim_r.at[0], after_id),
        remote(res_in.at[:, :width], rim_in.at[1], rim_s.at[1], rim_r.at[1], before_id),
    ]
    for copy in rims:
        copy.start()

    loads[0].wait()
    loads[1].wait()
    prepare_places(
        peers, capacity, spread, owner, slot, local, pos_hi, pos_hi16, hot_el, slot_buf
    )
    loads[2].wait()
    nodes = stiff.shape[0]
    keep_parts(wa, pi_weights(pi[:128], 2, nodes))
    keep_parts(wb, pi_weights(pi[128:], 8, nodes))

    def hot_edges(i, _):
        at = pl.ds(pl.multiple_of(i * WIDE, WIDE), WIDE)
        index = emap[:, at]
        emap_hi[:, at] = index // CHUNK
        emap_hi16[:, at] = wide16(index // CHUNK)
        hot_ed[:, at] = onehot(index % CHUNK)
        return 0

    lax.fori_loop(0, emap.shape[1] // WIDE, hot_edges, 0)
    loads[3].wait()
    for copy in rims:
        copy.wait_recv()

    def send_aux():
        loads[4].wait()
        loads[5].wait()
        prepare_coefs(coef, stiff, mass, coef_q, diag_q)
        scatter_elems(diag_q, pos_hi16, hot_el, acc_d)
        for g in range(slot_buf.shape[0]):
            acc_d[g * AUX + 3 : g * AUX + 4, :] = slot_buf[g : g + 1, :]
        lay_out(aux_send, acc_d, AUX)
        each_peer(lambda d: to_peer(aux_send, aux_recv, aux_s, aux_r, d).start())

    def restrict_half(half):
        mine = slice(half * rhs, (half + 1) * rhs)
        e_table[...] = jnp.zeros_like(e_table)
        blocks = [res[mine, i * CHUNK : (i + 1) * CHUNK] for i in range(edges // CHUNK)]
        for side in range(2):
            for i in range(width // CHUNK):
                blocks.append(rim_in[side, mine, i * CHUNK : (i + 1) * CHUNK])
        for h, block in enumerate(blocks):
            e_table[h * rhs : (h + 1) * rhs, :] = block
        e_table2[...] = split_wide(e_table[...])
        edge_gather(e_table2, emap_hi, hot_ed, e_groups, rhs, xa, xb)
        restrict(xa, xb, wa, wb, rhs, terms)
        scatter_elems(terms, pos_hi16, hot_el, acc)
        lay_out(send.at[0, half], acc, rows)
        each_peer(lambda d: to_peer(*refs(0, half), d).start())

    def learn_home():
        floored[...] = jnp.zeros_like(floored)
        flag[...] = jnp.zeros_like(flag)

        def learn(got, s):
            row = got[s, 3:4, :]
            flag[...] = jnp.maximum(flag[...], jnp.max(row, axis=1, keepdims=True))
            high, low = home_index(row)
            hot = onehot(low)
            home_hi[s] = high
            hot_home[s] = hot
            high16 = wide16(high)
            home_hi16[s] = high16
            values = jnp.concatenate([got[s], jnp.zeros_like(got[s])], axis=0)
            add_parts(floored, scatter_cols(values, high16, hot, home), AUX)

        def other(d):
            learn(aux_recv, wait_from(aux_send, aux_recv, aux_s, aux_r, d))

        learn(aux_send, me)
        each_peer(other)
        floored[...] = jnp.maximum(floored[...], 1.0)
        for copy in flags:
            copy.start()

    def home_sum(stage, half, total):
        src, dst, ssem, rsem = refs(stage, half)
        add_parts(total, scatter_cols(src[me], home_hi16[me], hot_home[me], home), rows, True)

        def other(d):
            s = wait_from(src, dst, ssem, rsem, d)
            add_parts(total, scatter_cols(dst[s], home_hi16[s], hot_home[s], home), rows)

        each_peer(other)

    def home_values(h, c, half, second):
        at = slice(h * rows + c * rhs, h * rows + (c + 1) * rhs)
        weight = floored[h * AUX + c : h * AUX + c + 1, :]
        nodes = rhs_nodes[half, at, :]
        value = first * nodes / weight
        if second:
            value = keep * value + step * (nodes - h_acc[at, :]) / weight
        h_table[at, :] = value

    def home_half(stage, half, second):
        home_sum(stage, half, h_acc if second else rhs_nodes.at[half])
        h_table[...] = jnp.zeros_like(h_table)
        for h in range(home):
            for c in range(3):
                home_values(h, c, half, second)
        h_table2[...] = split_wide(h_table[...])
        src, dst, ssem, rsem = refs(stage + 1, half)

        def reply(d):
            peer = partner(d)
            src[peer] = gather_cols(h_table2[...], home_hi[peer], hot_home[peer], home, rows)
            to_peer(src, dst, ssem, rsem, d).start()

        each_peer(reply)
        dst[me] = gather_cols(h_table2[...], home_hi[me], hot_home[me], home, rows)

    def fetched(stage, half):
        each_peer(lambda d: wait_from(*refs(stage, half), d))
        table_from(recv.at[stage, half], rows, n_table, n_table2)

    def operate_half(half):
        fetched(1, half)

        def visit(i, value):
            for s in range(2):
                at = pl.multiple_of((2 * i + s) * rows, rows)
                x_all[pl.ds(at, rows), :] = value[:, s * CHUNK : (s + 1) * CHUNK]

        gather_elems(n_table2, pos_hi, hot_el, rows, visit)
        apply_operator(x_all, ws, wm, coef_q, rhs, terms)
        scatter_elems(terms, pos_hi16, hot_el, acc)
        lay_out(send.at[2, half], acc, rows)
        each_peer(lambda d: to_peer(*refs(2, half), d).start())

    def backs(half):
        return [
            remote(
                rim_out.at[half, 0], rim_back.at[half, 1], back_s.at[half, 0],
                back_r.at[half, 0], before_id,
            ),
            remote(
                rim_out.at[half, 1], rim_back.at[half, 0], back_s.at[half, 1],
                back_r.at[half, 1], after_id,
            ),
        ]

    def prolong_half(half):
        fetched(3, half)

        def visit(i, value):
            for c in range(3):
                part = value[c * rhs : (c + 1) * rhs]
                x3b[pl.ds(pl.multiple_of(i * rhs, rhs), rhs), c * WIDE : (c + 1) * WIDE] = part
                for s in range(4):
                    at = pl.multiple_of((4 * i + s) * rhs, rhs)
                    x3a[pl.ds(at, rhs), c * 128 : (c + 1) * 128] = part[:, s * 128 : (s + 1) * 128]

        gather_elems(n_table2, pos_hi, hot_el, rows, visit)
        ea[...] = dot3_nt(x3a[...], wa[0], wa[1])
        eb[...] = dot3_nt(x3b[...], wb[0], wb[1])
        edge_scatter(ea, eb, emap_hi16, hot_ed, rhs, e_acc.at[half])
        h = edges // CHUNK
        for side in range(2):
            for i in range(width // CHUNK):
                rim_out[half, side, :, i * CHUNK : (i + 1) * CHUNK] = e_acc[
                    half, h * rhs : (h + 1) * rhs, :
                ]
                h += 1
        for copy in backs(half):
            copy.start()

    restrict_half(0)
    send_aux()
    restrict_half(1)
    keep_parts(ws, block_weights(stiff[...], 4))
    keep_parts(wm, block_weights(mass[...], 4))
    learn_home()
    home_half(0, 0, False)
    home_half(0, 1, False)
    operate_half(0)
    operate_half(1)
    home_half(2, 0, True)
    home_half(2, 1, True)
    prolong_half(0)
    prolong_half(1)

    count, reach = edges // CHUNK, width // CHUNK
    for half in range(2):
        mine = slice(half * rhs, (half + 1) * rhs)
        for copy in backs(half):
            copy.wait_recv()
        for h in range(count):
            value = e_acc[half, h * rhs : (h + 1) * rhs, :]
            if h < reach:
                value = value + rim_back[half, 0, :, h * CHUNK : (h + 1) * CHUNK]
            if h >= count - reach:
                at = (h - count + reach) * CHUNK
                value = value + rim_back[half, 1, :, at : at + CHUNK]
            out[mine, h * CHUNK : (h + 1) * CHUNK] = value

    worst = flag[...]
    for i, copy in enumerate(flags):
        copy.wait_recv()
        worst = jnp.maximum(worst, flag_in[i])
    flag_out[...] = worst
    for copy in rims + backs(0) + backs(1) + flags:
        copy.wait_send()

    def sent(d):
        to_peer(aux_send, aux_recv, aux_s, aux_r, d).wait_send()
        for stage in range(4):
            for half in range(2):
                to_peer(*refs(stage, half), d).wait_send()

    each_peer(sent)


def per_device(
    residual, pi, stiff, mass, permittivity, curl, edge_map, local_map, node_owner, node_slot
):
    rhs, edges = residual.shape
    ed, elems = edge_map.shape
    nodes = local_map.shape[0]
    touched = node_owner.shape[0]
    peers, grps = lax.axis_size("dev"), lax.axis_size("grp")
    rim = edges // 8
    width = -(-rim // CHUNK) * CHUNK
    place = edge_map.T - rim
    place = jnp.where(
        place < 0,
        place + edges + width,
        jnp.where(place >= edges, place + width, place),
    )
    emap = jnp.concatenate([place[:, :128].reshape(1, -1), place[:, 128:].reshape(1, -1)], axis=1)
    local = local_map.T.reshape(1, -1)
    coef = jnp.concatenate([curl[None], permittivity, jnp.zeros((1, elems), F32)], axis=0)
    args = (residual, emap, local, node_owner[None], node_slot[None], coef, pi, stiff, mass)
    most = 2 * touched // peers
    usual = -(-(3 * touched // (2 * peers)) // 128) * 128
    if usual >= most:
        return run(grps, peers, ed, elems, nodes, touched, most, False, args)[0]
    result, flag = run(grps, peers, ed, elems, nodes, touched, usual, True, args)

    def with_room(result, *args):
        return run(grps, peers, ed, elems, nodes, touched, most, False, args)[0]

    return lax.cond(flag[0, 0] >= FULL, with_room, lambda result, *args: result, result, *args)


def run(grps, peers, ed, elems, nodes, touched, capacity, spread, args):
    residual, pi, stiff, mass = args[0], args[6], args[7], args[8]
    rhs, edges = residual.shape
    width = -(-(edges // 8) // CHUNK) * CHUNK
    entries = nodes * elems
    groups = peers * capacity // CHUNK
    home = -(-N_LOC // CHUNK)
    home_even = home + home % 2
    e_groups = (edges + 2 * width) // CHUNK
    e_even = e_groups + e_groups % 2
    pairs, eights = elems // 2, elems // 8
    half = rhs // 2
    rows = 3 * half
    scratch = [
        ((rhs, edges), F32),
        ((1, touched), jnp.int32),
        ((1, touched), jnp.int32),
        (pi.shape, F32),
        (stiff.shape, F32),
        (mass.shape, F32),
        ((2, rhs, width), F32),
        ((2, 2, half, width), F32),
        ((2, 2, half, width), F32),
        ((peers, AUX // 2, capacity), F32),
        ((peers, AUX // 2, capacity), F32),
        ((4, 2, peers, rows, capacity), F32),
        ((4, 2, peers, rows, capacity), F32),
        ((CHUNK, entries), BF16),
        ((CHUNK, ed * elems), BF16),
        ((peers, CHUNK, capacity), BF16),
        ((1, ed * elems), jnp.int32),
        ((1, entries), jnp.int32),
        ((peers, 1, capacity), jnp.int32),
        ((16, ed * elems), jnp.int16),
        ((16, entries), jnp.int16),
        ((peers, 16, capacity), jnp.int16),
        ((groups, CHUNK), F32),
        ((AUX, entries), F32),
        ((AUX, entries), F32),
        ((2, 256, 384), BF16),
        ((2, 128, 1536), BF16),
        ((2, CHUNK, CHUNK), BF16),
        ((2, CHUNK, CHUNK), BF16),
        ((e_even * half, CHUNK), F32),
        ((e_even * half, 2 * CHUNK), BF16),
        ((pairs * half, 256), F32),
        ((eights * half, 128), F32),
        ((pairs * half, 384), F32),
        ((eights * half, 1536), F32),
        ((pairs * half, 256), F32),
        ((eights * half, 128), F32),
        ((rows, entries), F32),
        ((groups * rows, CHUNK), F32),
        ((groups * rows, 2 * CHUNK), BF16),
        ((entries // CHUNK * rows, CHUNK), F32),
        ((groups * rows, CHUNK), F32),
        ((groups * AUX, CHUNK), F32),
        ((home_even * rows, CHUNK), F32),
        ((home_even * rows, 2 * CHUNK), BF16),
        ((2, home * rows, CHUNK), F32),
        ((home * rows, CHUNK), F32),
        ((home * AUX, CHUNK), F32),
        ((2, e_groups * half, CHUNK), F32),
        ((8, 128), F32),
        ((grps - 1, 8, 128), F32),
    ]
    sems = [(2,), (2,), (peers,), (peers,), (4, 2, peers), (4, 2, peers), (2, 2), (2, 2), (6,), (grps - 1,), (grps - 1,)]
    vmem, where = pl.BlockSpec(memory_space=pltpu.VMEM), pl.BlockSpec(memory_space=pl.ANY)
    return pl.pallas_call(
        functools.partial(kernel, grps, peers, home, e_groups, capacity, spread),
        out_shape=[
            jax.ShapeDtypeStruct((rhs, edges), F32), jax.ShapeDtypeStruct((8, 128), F32)
        ],
        in_specs=[where, vmem, vmem, where, where, vmem, where, where, where],
        out_specs=[vmem, vmem],
        scratch_shapes=[pltpu.VMEM(*s) for s in scratch]
        + [pltpu.SemaphoreType.DMA(s) for s in sems],
        compiler_params=pltpu.CompilerParams(
            collective_id=0 if spread else 1, has_side_effects=True, vmem_limit_bytes=VMEM_BYTES
        ),
    )(*args)


def solution(mesh):
    both = ("grp", "dev")
    in_specs = (
        P(None, both), P(), P(), P(), P(None, both), P(both), P(None, both), P(None, both),
        P(both), P(both),
    )
    return jax.shard_map(
        per_device, mesh=mesh, in_specs=in_specs, out_specs=P(None, both), check_vma=False
    )
```
